32 devices in a mesh: batch: 4 (over x, core), ctx: 8 (over z, y).
Axes of the slice: x: 2, y: 2, z: 4, core: 2. Of those that a mesh axis runs over, the one named last changes fastest.
Arguments:
- lengths: int32 [64], P('batch'), parts along dimension 0, may hold values from 1 to 2560, 4096 in all
- queries: bfloat16 [16384, 512], P(('batch', 'ctx')), parts along dimension 0, may hold values from -256 to 256
- key_rows: bfloat16 [16384, 128], P(('batch', 'ctx')), parts along dimension 0, may hold values from -4.5 to 4.5
- values: bfloat16 [16384, 128], P(('batch', 'ctx')), parts along dimension 0, may hold values from -6 to 6
Outputs:
- attended: bfloat16 [16384, 512], P(('batch', 'ctx')), parts along dimension 0
- log_mass: float32 [4, 16384], P(None, ('batch', 'ctx')), parts along dimension 1
The draws below stay inside these ranges and needn't reach their ends.
There are 4 independent parts, one for each index of `batch`. The reference program is written for one: setup_inputs(seed, part) draws one part's arguments, and reference() takes and returns one part's arrays. A program takes and returns all parts, laid end to end along the dimension named above; each array names one. Nothing has to cross between parts.
Inputs may be any that keep to these rules, and one draw needn't show every extreme that they name: The lengths sum to 4096; the longest is exactly 2560.
All inputs are finite; a program needn't handle non-finite values.
Results may differ from the reference program's by a relative error of at most 0.0035.
Values may be sent and summed in bfloat16 or wider, within the bound.
No kernel may reach another device: no remote copies, remote signals or barrier semaphores. Data moves between devices by JAX's collectives and lax.ppermute only.
A program may use at most 64 MiB of HBM per device.

```python
import math
import jax
import jax.numpy as jnp
import numpy as np
from jax import lax

QH = 4
HD = 128
DOCS = 16
SEQ = 4096
MOST = 2560


def drawn_keys(key):
    seeded = jax.random.fold_in(key, 17)
    drawn = jnp.clip(jax.random.normal(seeded, (SEQ, HD), jnp.float32), -4.5, 4.5)
    return drawn


def draw_key_rows(key, part):
    return drawn_keys(key).astype(jnp.bfloat16)


def draw_queries(key, part):
    seeded = jax.random.fold_in(key, 23)
    background = jnp.clip(1.5 * jax.random.normal(seeded, (SEQ, QH * HD), jnp.float32), -9.0, 9.0)
    return background.astype(jnp.bfloat16)


def block_scale(rng, dims, shards, least, largest):
    def one(dim, blocks):
        heights = jax.random.uniform(jax.random.fold_in(jax.random.fold_in(rng, 6), dim), (blocks,), jnp.float32, least / len(shards), largest / len(shards))
        return jnp.repeat(jnp.exp(heights), dims[dim] // blocks).reshape((-1,) + (1,) * (len(dims) - dim - 1))

    loudness = one(*shards[0])
    for cut in shards[1:]:
        loudness = loudness * one(*cut)
    return loudness


def length_profile(count, total, most, lean):
    loads = [(1 << 20) // math.isqrt(standing ** lean) + 1 for standing in range(2, count + 1)]
    spare, counts = total - most - (count - 1), [1] * (count - 1)
    while spare > 0:
        movable = [i for i in range(count - 1) if counts[i] < most]
        pool, remaining = sum([loads[i] for i in movable]), spare
        for i in movable:
            extra = min(most - counts[i], max(1, remaining * loads[i] // pool), spare)
            counts[i] = counts[i] + extra
            spare = spare - extra
    return np.array([most] + counts)


def uneven_parts(stream_key, number_of, total, reach, skew):
    if number_of == 2:
        one = jax.random.randint(stream_key, (), max(1, total - reach), min(reach, total - 1) + 1)
        return jnp.stack([one, total - one])
    sizes = jnp.asarray(length_profile(number_of, total, reach, skew), jnp.int32)
    twos = (number_of - 1) // 2
    source_of, sink = sizes[1:1 + 2 * twos:2], sizes[2:2 + 2 * twos:2]
    margin = jnp.minimum(source_of - 1, reach - sink)
    shifted = jax.random.randint(jax.random.fold_in(stream_key, 1), (twos,), 0, 1 << 20) % (margin + 1)
    sizes = sizes.at[1:1 + 2 * twos:2].set(source_of - shifted).at[2:2 + 2 * twos:2].set(sink + shifted)
    return sizes[jax.random.permutation(jax.random.fold_in(stream_key, 2), number_of)]


def gaussian(stream_key, dims, scale, bound, pieces=(), held_as=jnp.bfloat16):
    result = jax.random.normal(stream_key, dims, jnp.float32) * scale
    if len(pieces) > 0:
        result = block_scale(stream_key, dims, pieces, -0.22, 0.18) * result
    return jnp.clip(result, min=-bound, max=bound).astype(held_as)


def setup_inputs(seed: int = 0, part: int = 0) -> dict:
    seeds = jax.random.split(jax.random.key(seed), 5)
    part_splits = jax.random.split(jax.random.fold_in(seeds[4], part), 5)
    return {
        "lengths": uneven_parts(part_splits[0], DOCS, SEQ, MOST, 2).astype(jnp.int32),
        "queries": draw_queries(jax.random.fold_in(jax.random.fold_in(seeds[4], part), 71), part),
        "key_rows": draw_key_rows(jax.random.fold_in(jax.random.fold_in(seeds[4], part), 71), part),
        "values": gaussian(part_splits[3], (SEQ, HD), 1.0, 6.0, ((0, 8),)),
    }


def doc_numbers(lengths, positions):
    doc_ends = jnp.cumsum(lengths).astype(jnp.int32)
    return jnp.sum((positions[:, None] >= doc_ends[None, :]).astype(jnp.int32), axis=1)


def reference(lengths, queries, key_rows, values):
    all_pos = jnp.arange(SEQ, dtype=jnp.int32)
    doc_index = doc_numbers(lengths, all_pos)
    block_rows = min(512, SEQ)
    block_count = SEQ // block_rows
    query_blocks = queries.reshape(block_count, block_rows, QH, HD)
    first_rows = (jnp.arange(block_count, dtype=jnp.int32) * block_rows).astype(jnp.int32)
    score_scale = 1.0 / (HD ** 0.5)
    keys_wide = key_rows.astype(jnp.float32)
    values_wide = values.astype(jnp.float32)

    def attend_block(packed):
        query_block, first_row = packed
        q_pos = first_row + jnp.arange(block_rows, dtype=jnp.int32)
        q_doc = lax.dynamic_slice_in_dim(doc_index, first_row, block_rows, 0)
        visible = (q_doc[:, None] == doc_index[None, :]) & (all_pos[None, :] <= q_pos[:, None])
        scores = jnp.einsum('thd,kd->htk', query_block.astype(jnp.float32), keys_wide) * score_scale
        scores = jnp.where(visible[None], scores, -1e30)
        row_max = jnp.max(scores, axis=2)
        weights = jnp.where(visible[None], jnp.exp(scores - row_max[:, :, None]), 0.0)
        total = jnp.sum(weights, axis=2)
        weight_bf = weights.astype(jnp.bfloat16)
        mixed = jnp.einsum('htk,kd->thd', weight_bf.astype(jnp.float32), values_wide)
        mixed = mixed / jnp.transpose(total)[:, :, None]
        attended = mixed.reshape(block_rows, QH * HD).astype(jnp.bfloat16)
        return attended, row_max + jnp.log(total)

    attended, log_mass = lax.map(attend_block, (query_blocks, first_rows))
    attended = attended.reshape(SEQ, QH * HD)
    log_mass = jnp.transpose(log_mass, (1, 0, 2)).reshape(QH, SEQ)
    return attended, log_mass
```

```python
import functools
import math

import jax
import jax.numpy as jnp
from jax import lax
from jax.experimental import pallas as pl
from jax.experimental.pallas import tpu as pltpu
from jax.sharding import PartitionSpec as P

QH = 4
HD = 128
LOW = -1e30
SCALE = 1.0 / math.sqrt(HD)
EXP2_SCALE = SCALE * math.log2(math.e)
VMEM_LIMIT = 56 * 1024 * 1024


def scores_of(heads, keys):
    return lax.dot_general(
        heads, keys, (((1,), (1,)), ((), ())), preferred_element_type=jnp.float32
    )


def stacked_heads(q_ref, rows):
    return jnp.concatenate([q_ref[rows, h * HD : (h + 1) * HD] for h in range(QH)], axis=0)


def lane_parts(tile, combine):
    parts = [tile[:, c : c + HD] for c in range(0, tile.shape[1], HD)]
    return functools.reduce(combine, parts)


def own_kernel(lengths_ref, q_ref, k_ref, v_ref, acc_ref, max_ref, sum_ref):
    q_rows = q_ref.shape[0]
    tile = math.gcd(q_rows, 128)
    own_first = lax.axis_index("ctx") * q_rows
    ends = []
    end = jnp.int32(0)
    for d in range(lengths_ref.shape[0]):
        end = end + lengths_ref[d]
        ends.append(end - own_first)
    for t in range(q_rows // tile):
        keys = (t + 1) * tile
        row = lax.broadcasted_iota(jnp.int32, (tile, HD), 0) + t * tile
        start = jnp.zeros((tile, HD), jnp.int32)
        for end in ends:
            start = jnp.where(row >= end, jnp.maximum(start, end), start)
        start = jnp.concatenate([start] * (keys // HD), axis=1)
        row = lax.broadcasted_iota(jnp.int32, (tile, keys), 0) + t * tile
        key = lax.broadcasted_iota(jnp.int32, (tile, keys), 1)
        hidden = (key < start) | (key > row)
        heads = stacked_heads(q_ref, slice(t * tile, (t + 1) * tile))
        scores = scores_of(heads, k_ref[:keys, :])
        scores = jnp.where(jnp.concatenate([hidden] * QH, axis=0), LOW, scores)
        top = jnp.max(scores, axis=1, keepdims=True)
        weights = jnp.exp2((scores - top) * EXP2_SCALE)
        total = jnp.sum(weights, axis=1, keepdims=True)
        mixed = jnp.dot(
            weights.astype(jnp.bfloat16), v_ref[:keys, :], preferred_element_type=jnp.float32
        )
        for h in range(QH):
            rows = slice(h * tile, (h + 1) * tile)
            here = slice(t * tile, (t + 1) * tile)
            acc_ref[h, here, :] = mixed[rows]
            max_ref[h, here, :] = jnp.broadcast_to(top[rows], (tile, HD))
            sum_ref[h, here, :] = jnp.broadcast_to(total[rows], (tile, HD))


def past_kernel(
    tile,
    lengths_ref,
    q_ref,
    acc_ref,
    max_ref,
    sum_ref,
    kg_ref,
    vg_ref,
    out_ref,
    mass_ref,
    k_buf,
    v_buf,
    s_buf,
    k_sem,
    v_sem,
):
    q_rows = q_ref.shape[0]
    here = lax.axis_index("ctx")
    own_first = here * q_rows
    first = jnp.int32(0)
    last = jnp.int32(0)
    end = jnp.int32(0)
    for d in range(lengths_ref.shape[0]):
        begin, end = end, end + lengths_ref[d]
        holds = (begin < own_first) & (end > own_first)
        first = jnp.where(holds, begin, first)
        last = jnp.where(holds, end, last)
    live_rows = jnp.clip(last - own_first, 0, q_rows)
    first_block = jnp.where(live_rows > 0, first // q_rows, here)
    blocks = here - first_block
    cut = first - first_block * q_rows

    def copies(b):
        rows = pl.ds((first_block + b) * q_rows, q_rows)
        return (
            pltpu.make_async_copy(kg_ref.at[rows, :], k_buf.at[b], k_sem.at[b]),
            pltpu.make_async_copy(vg_ref.at[rows, :], v_buf.at[b], v_sem.at[b]),
        )

    def start_block(b, _):
        k_copy, v_copy = copies(b)
        k_copy.start()
        v_copy.start()
        return 0

    lax.fori_loop(0, blocks, start_block, 0)

    def wait_block(b, _):
        k_copy, v_copy = copies(b)
        k_copy.wait()
        v_copy.wait()
        return 0

    lax.fori_loop(0, blocks, wait_block, 0)

    def finish(rows_at, top, total, mixed):
        lane = lax.broadcasted_iota(jnp.int32, (tile, HD), 1)
        mass = top * SCALE + jnp.log(total)
        packed = jnp.zeros((tile, HD), jnp.float32)
        out = mixed / total
        for h in range(QH):
            part = slice(h * tile, (h + 1) * tile)
            out_ref[rows_at, h * HD : (h + 1) * HD] = out[part].astype(jnp.bfloat16)
            packed = jnp.where(lane == h, mass[part], packed)
        for c in range(0, tile, HD):
            turned = jnp.transpose(packed[c : c + HD])
            mass_ref[:, pl.ds(pl.multiple_of(rows_at.start + c, HD), HD)] = turned[:QH, :]

    def per_tile(t, _):
        rows_at = pl.ds(pl.multiple_of(t * tile, tile), tile)
        old_top = jnp.concatenate([max_ref[h, rows_at, :] for h in range(QH)], axis=0)
        old_total = jnp.concatenate([sum_ref[h, rows_at, :] for h in range(QH)], axis=0)
        old_mixed = jnp.concatenate([acc_ref[h, rows_at, :] for h in range(QH)], axis=0)
        seen = (t * tile < live_rows) & (blocks > 0)

        @pl.when(seen)
        def _():
            heads = stacked_heads(q_ref, rows_at)

            def score_block(b, top):
                scores = scores_of(heads, k_buf[b])
                key = lax.broadcasted_iota(jnp.int32, (1, q_rows), 1) + b * q_rows
                scores = jnp.where(key < cut, LOW, scores)
                s_buf[b] = scores
                return jnp.maximum(top, lane_parts(scores, jnp.maximum))

            top = lax.fori_loop(
                0, blocks, score_block, jnp.full((QH * tile, HD), LOW, jnp.float32)
            )
            row = lax.broadcasted_iota(jnp.int32, (tile, HD), 0) + t * tile
            live = jnp.concatenate([row < live_rows] * QH, axis=0)
            top = jnp.broadcast_to(jnp.max(top, axis=1, keepdims=True), top.shape)
            top = jnp.maximum(old_top, jnp.where(live, top, LOW))
            top_wide = jnp.concatenate([top] * (q_rows // HD), axis=1)

            def mix_block(b, carried):
                total, mixed = carried
                weights = jnp.exp2((s_buf[b] - top_wide) * EXP2_SCALE)
                total = total + lane_parts(weights, jnp.add)
                mixed = mixed + jnp.dot(
                    weights.astype(jnp.bfloat16), v_buf[b], preferred_element_type=jnp.float32
                )
                return total, mixed

            zero = jnp.zeros((QH * tile, HD), jnp.float32)
            total, mixed = lax.fori_loop(0, blocks, mix_block, (zero, zero))
            total = jnp.broadcast_to(jnp.sum(total, axis=1, keepdims=True), total.shape)
            decay = jnp.exp2((old_top - top) * EXP2_SCALE)
            total = old_total * decay + jnp.where(live, total, 0.0)
            mixed = old_mixed * decay + jnp.where(live, mixed, 0.0)
            finish(rows_at, top, total, mixed)

        @pl.when(jnp.logical_not(seen))
        def _():
            finish(rows_at, old_top, old_total, old_mixed)

        return 0

    lax.fori_loop(0, q_rows // tile, per_tile, 0)


def on_device(lengths, queries, key_rows, values):
    q_rows = queries.shape[0]
    ctx_count = lax.axis_size("ctx")
    reach = min(ctx_count // 2 + 1, ctx_count - 1)
    in_smem = pl.BlockSpec(memory_space=pltpu.SMEM)
    in_vmem = pl.BlockSpec(memory_space=pltpu.VMEM)
    in_any = pl.BlockSpec(memory_space=pl.ANY)
    params = pltpu.CompilerParams(vmem_limit_bytes=VMEM_LIMIT)
    state = jax.ShapeDtypeStruct((QH, q_rows, HD), jnp.float32)

    all_keys = lax.all_gather(key_rows, "ctx", axis=0, tiled=True)
    all_values = lax.all_gather(values, "ctx", axis=0, tiled=True)
    acc, top, total = pl.pallas_call(
        own_kernel,
        out_shape=(state, state, state),
        in_specs=[in_smem, in_vmem, in_vmem, in_vmem],
        out_specs=(in_vmem, in_vmem, in_vmem),
        compiler_params=params,
        cost_estimate=pl.CostEstimate(
            flops=4 * QH * q_rows * q_rows * HD,
            bytes_accessed=8 * q_rows * QH * HD,
            transcendentals=QH * q_rows * q_rows,
        ),
    )(lengths, queries, key_rows, values)
    tile = math.gcd(q_rows, 256)
    return pl.pallas_call(
        functools.partial(past_kernel, tile),
        out_shape=(
            jax.ShapeDtypeStruct((q_rows, QH * HD), jnp.bfloat16),
            jax.ShapeDtypeStruct((QH, q_rows), jnp.float32),
        ),
        in_specs=[in_smem, in_vmem, in_vmem, in_vmem, in_vmem, in_any, in_any],
        out_specs=(in_vmem, in_vmem),
        scratch_shapes=[
            pltpu.VMEM((reach, q_rows, HD), jnp.bfloat16),
            pltpu.VMEM((reach, q_rows, HD), jnp.bfloat16),
            pltpu.VMEM((reach, QH * tile, q_rows), jnp.float32),
            pltpu.SemaphoreType.DMA((reach,)),
            pltpu.SemaphoreType.DMA((reach,)),
        ],
        compiler_params=params,
    )(lengths, queries, acc, top, total, all_keys, all_values)


def solution(mesh):
    in_specs = (
        P("batch"),
        P(("batch", "ctx"), None),
        P(("batch", "ctx"), None),
        P(("batch", "ctx"), None),
    )
    out_specs = (P(("batch", "ctx"), None), P(None, ("batch", "ctx")))
    return jax.shard_map(
        on_device, mesh=mesh, in_specs=in_specs, out_specs=out_specs, check_vma=False
    )
```

```python
import functools
import math

import jax
import jax.numpy as jnp
from jax import lax
from jax.experimental import pallas as pl
from jax.experimental.pallas import tpu as pltpu
from jax.sharding import PartitionSpec as P

QH = 4
HD = 128
LOW = -1e30
SCALE = 1.0 / math.sqrt(HD)
EXP2_SCALE = SCALE * math.log2(math.e)
VMEM_LIMIT = 32 * 1024 * 1024


def scores_of(heads, keys):
    return lax.dot_general(
        heads, keys, (((1,), (1,)), ((), ())), preferred_element_type=jnp.float32
    )


def lane_parts(tile, combine):
    parts = [tile[:, c : c + HD] for c in range(0, tile.shape[1], HD)]
    return functools.reduce(combine, parts)


def packed_lanes(columns, lane):
    packed = jnp.zeros(lane.shape, jnp.float32)
    for n, column in enumerate(columns):
        packed = jnp.where(lane == n, column, packed)
    return packed


def own_kernel(lengths_ref, q_ref, k_ref, v_ref, acc_ref, stat_ref):
    q_rows = q_ref.shape[0]
    tile = math.gcd(q_rows, 128)
    own_first = lax.axis_index("ctx") * q_rows
    ends = []
    end = jnp.int32(0)
    for d in range(lengths_ref.shape[0]):
        end = end + lengths_ref[d]
        ends.append(end - own_first)
    for t in range(q_rows // tile):
        keys = (t + 1) * tile
        here = slice(t * tile, (t + 1) * tile)
        row = lax.broadcasted_iota(jnp.int32, (tile, HD), 0) + t * tile
        start = jnp.zeros((tile, HD), jnp.int32)
        for end in ends:
            start = jnp.where(row >= end, jnp.maximum(start, end), start)
        start = jnp.concatenate([start] * (keys // HD), axis=1)
        row = lax.broadcasted_iota(jnp.int32, (tile, keys), 0) + t * tile
        key = lax.broadcasted_iota(jnp.int32, (tile, keys), 1)
        hidden = (key < start) | (key > row)
        heads = jnp.concatenate([q_ref[here, h * HD : (h + 1) * HD] for h in range(QH)], axis=0)
        scores = scores_of(heads, k_ref[:keys, :])
        scores = jnp.where(jnp.concatenate([hidden] * QH, axis=0), LOW, scores)
        top = jnp.max(scores, axis=1, keepdims=True)
        weights = jnp.exp2((scores - top) * EXP2_SCALE)
        total = jnp.sum(weights, axis=1, keepdims=True)
        mixed = jnp.dot(
            weights.astype(jnp.bfloat16), v_ref[:keys, :], preferred_element_type=jnp.float32
        )
        parts = [slice(h * tile, (h + 1) * tile) for h in range(QH)]
        for h in range(QH):
            acc_ref[h, here, :] = mixed[parts[h]]
        columns = [top[p] for p in parts] + [total[p] for p in parts]
        stat_ref[here, :] = packed_lanes(columns, lax.broadcasted_iota(jnp.int32, (tile, HD), 1))


def past_kernel(distances, is_last, lengths_ref, q_ref, acc_in, stat_in, *refs):
    kv_refs = refs[: len(distances)]
    first_out, second_out = refs[len(distances) : len(distances) + 2]
    acc_ref, stat_ref = refs[len(distances) + 2 :] if is_last else (first_out, second_out)
    tile = q_ref.shape[0]
    shard_rows = kv_refs[0].shape[1]
    here = lax.axis_index("ctx")
    odd = here % 2
    own_first = here * shard_rows
    first = own_first
    last = own_first
    end = jnp.int32(0)
    for d in range(lengths_ref.shape[0]):
        begin, end = end, end + lengths_ref[d]
        holds = (begin < own_first) & (end > own_first)
        first = jnp.where(holds, begin, first)
        last = jnp.where(holds, end, last)
    first_row = pl.program_id(0) * tile
    live_rows = last - own_first - first_row

    acc_ref[...] = acc_in[...]
    stat_ref[...] = stat_in[...]
    lane = lax.broadcasted_iota(jnp.int32, (tile, HD), 1)

    def absorb(kv_ref, cut):
        key = lax.broadcasted_iota(jnp.int32, (1, shard_rows), 1)
        live = lax.broadcasted_iota(jnp.int32, (tile, HD), 0) < live_rows
        keys = kv_ref[0]
        shard_values = kv_ref[1]
        tops, totals = [], []
        for h in range(QH):
            scores = scores_of(q_ref[:, h * HD : (h + 1) * HD], keys)
            scores = jnp.where(key < cut, LOW, scores)
            old_top = jnp.broadcast_to(stat_ref[:, h : h + 1], (tile, HD))
            old_total = jnp.broadcast_to(stat_ref[:, QH + h : QH + h + 1], (tile, HD))
            top = jnp.max(lane_parts(scores, jnp.maximum), axis=1, keepdims=True)
            top = jnp.where(live, jnp.maximum(old_top, top), old_top)
            wide = jnp.concatenate([top] * (shard_rows // HD), axis=1)
            weights = jnp.exp2((scores - wide) * EXP2_SCALE)
            total = jnp.sum(lane_parts(weights, jnp.add), axis=1, keepdims=True)
            mixed = jnp.dot(
                weights.astype(jnp.bfloat16), shard_values, preferred_element_type=jnp.float32
            )
            decay = jnp.exp2((old_top - top) * EXP2_SCALE)
            acc_ref[h] = acc_ref[h] * decay + jnp.where(live, mixed, 0.0)
            tops.append(top)
            totals.append(old_total * decay + jnp.where(live, total, 0.0))
        stat_ref[...] = packed_lanes(tops + totals, lane)

    for kv_ref, (even_distance, odd_distance) in zip(kv_refs, distances):
        distance = jnp.where(odd == 1, odd_distance, even_distance)
        shard_first = (here - distance) * shard_rows
        seen = (distance > 0) & (live_rows > 0) & (first < shard_first + shard_rows)
        pl.when(seen)(functools.partial(absorb, kv_ref, first - shard_first))

    if is_last:
        columns = []
        for h in range(QH):
            top = jnp.broadcast_to(stat_ref[:, h : h + 1], (tile, HD))
            total = jnp.broadcast_to(stat_ref[:, QH + h : QH + h + 1], (tile, HD))
            first_out[:, h * HD : (h + 1) * HD] = (acc_ref[h] / total).astype(jnp.bfloat16)
            columns.append(top * SCALE + jnp.log(total))
        mass = packed_lanes(columns, lane)
        for c in range(0, tile, HD):
            second_out[:, c : c + HD] = jnp.transpose(mass[c : c + HD])[:QH, :]


def state_shapes(q_rows):
    return (
        jax.ShapeDtypeStruct((QH, q_rows, HD), jnp.float32),
        jax.ShapeDtypeStruct((q_rows, HD), jnp.float32),
    )


def own_part(lengths, queries, key_rows, values):
    q_rows = queries.shape[0]
    in_smem = pl.BlockSpec(memory_space=pltpu.SMEM)
    in_vmem = pl.BlockSpec(memory_space=pltpu.VMEM)
    return pl.pallas_call(
        own_kernel,
        out_shape=state_shapes(q_rows),
        in_specs=[in_smem, in_vmem, in_vmem, in_vmem],
        out_specs=(in_vmem, in_vmem),
        compiler_params=pltpu.CompilerParams(vmem_limit_bytes=VMEM_LIMIT),
        cost_estimate=pl.CostEstimate(
            flops=8 * QH * q_rows * q_rows * HD,
            bytes_accessed=8 * q_rows * QH * HD,
            transcendentals=QH * q_rows * q_rows,
        ),
    )(lengths, queries, key_rows, values)


def past_part(lengths, queries, state, shards, is_last=False):
    q_rows = queries.shape[0]
    tile = math.gcd(q_rows, 256)
    distances = [s[0] for s in shards]
    arrays = [s[1] for s in shards]
    in_smem = pl.BlockSpec(memory_space=pltpu.SMEM)
    acc_spec = pl.BlockSpec((QH, tile, HD), lambda t: (0, t, 0))
    stat_spec = pl.BlockSpec((tile, HD), lambda t: (t, 0))
    q_spec = pl.BlockSpec((tile, QH * HD), lambda t: (t, 0))
    kv_spec = pl.BlockSpec((2, q_rows, HD), lambda t: (0, 0, 0))
    if is_last:
        out_shape = (
            jax.ShapeDtypeStruct((q_rows, QH * HD), jnp.bfloat16),
            jax.ShapeDtypeStruct((QH, q_rows), jnp.float32),
        )
        out_specs = (q_spec, pl.BlockSpec((QH, tile), lambda t: (0, t)))
        scratch = [pltpu.VMEM((QH, tile, HD), jnp.float32), pltpu.VMEM((tile, HD), jnp.float32)]
    else:
        out_shape = state_shapes(q_rows)
        out_specs = (acc_spec, stat_spec)
        scratch = []
    return pl.pallas_call(
        functools.partial(past_kernel, distances, is_last),
        grid=(q_rows // tile,),
        out_shape=out_shape,
        in_specs=[in_smem, q_spec, acc_spec, stat_spec] + [kv_spec] * len(arrays),
        out_specs=out_specs,
        scratch_shapes=scratch,
        compiler_params=pltpu.CompilerParams(vmem_limit_bytes=VMEM_LIMIT),
        cost_estimate=pl.CostEstimate(
            flops=8 * QH * q_rows * q_rows * HD * len(arrays),
            bytes_accessed=16 * q_rows * QH * HD,
            transcendentals=QH * q_rows * q_rows * len(arrays),
        ),
    )(lengths, queries, *state, *arrays)


def on_device(lengths, queries, key_rows, values):
    count = lax.axis_size("ctx")
    reach = min(count // 2 + 1, count - 1)
    strides = reach // 2

    def send(value, pairs):
        return lax.ppermute(value, "ctx", pairs)

    own = jnp.stack([key_rows, values])
    moving = send(own, [(i, i + 2) for i in range(count - 2)])
    beside = send(own, [(i, i + 1) for i in range(0, count, 2)])
    state = own_part(lengths, queries, key_rows, values)
    side_distances = (0, 1)
    for k in range(1, strides + 1):
        arrived = moving
        shards = [((2 * k, 2 * k), arrived), (side_distances, beside)]
        if k < strides:
            moving = send(arrived, [(i, i + 2) for i in range(2 * k, count - 2)])
        exchange = [(i + 1, i) for i in range(2 * k, count, 2)]
        side_distances = (2 * k - 1, 0)
        if 2 * k + 1 <= reach:
            exchange += [(i, i + 1) for i in range(2 * k, count, 2)]
            side_distances = (2 * k - 1, 2 * k + 1)
        beside = send(arrived, exchange)
        state = past_part(lengths, queries, state, shards)
    shards = [(side_distances, beside)]
    if reach % 2 == 1:
        far = send(own, [(i, i + reach) for i in range(1, count - reach, 2)])
        shards.append(((reach, 0), far))
    return past_part(lengths, queries, state, shards, is_last=True)


def solution(mesh):
    in_specs = (
        P("batch"),
        P(("batch", "ctx"), None),
        P(("batch", "ctx"), None),
        P(("batch", "ctx"), None),
    )
    out_specs = (P(("batch", "ctx"), None), P(None, ("batch", "ctx")))
    return jax.shard_map(
        on_device, mesh=mesh, in_specs=in_specs, out_specs=out_specs, check_vma=False
    )
```

```python
import functools
import math

import jax
import jax.numpy as jnp
from jax import lax
from jax.experimental import pallas as pl
from jax.experimental.pallas import tpu as pltpu
from jax.sharding import PartitionSpec as P

QH = 4
HD = 128
LOW = -1e30
SCALE = 1.0 / math.sqrt(HD)
EXP2_SCALE = SCALE * math.log2(math.e)
VMEM_LIMIT = 32 * 1024 * 1024


def dot(a, b):
    return jnp.dot(a, b, preferred_element_type=jnp.float32)


def own_kernel(lengths_ref, q_ref, k_ref, v_ref, qt_ref, acc_ref, stat_ref):
    q_rows = q_ref.shape[0]
    tile = math.gcd(q_rows, 128)
    own_first = lax.axis_index("ctx") * q_rows
    ends = []
    end = jnp.int32(0)
    for d in range(lengths_ref.shape[0]):
        end = end + lengths_ref[d]
        ends.append(end - own_first)
    values_t = jnp.transpose(v_ref[...])
    for h in range(QH):
        qt_ref[h] = jnp.transpose(q_ref[:, h * HD : (h + 1) * HD])
    for t in range(q_rows // tile):
        keys = (t + 1) * tile
        here = slice(t * tile, (t + 1) * tile)
        row = lax.broadcasted_iota(jnp.int32, (1, tile), 1) + t * tile
        start = jnp.zeros((1, tile), jnp.int32)
        for end in ends:
            start = jnp.where(row >= end, jnp.maximum(start, end), start)
        key = lax.broadcasted_iota(jnp.int32, (keys, tile), 0)
        hidden = (key < start) | (key > row)
        hidden = jnp.concatenate([hidden] * QH, axis=1)
        heads = jnp.concatenate([qt_ref[h, :, here] for h in range(QH)], axis=1)
        scores = jnp.where(hidden, LOW, dot(k_ref[:keys, :], heads))
        top = jnp.max(scores, axis=0, keepdims=True)
        weights = jnp.exp2((scores - top) * EXP2_SCALE)
        total = jnp.sum(weights, axis=0, keepdims=True)
        mixed = dot(values_t[:, :keys], weights.astype(jnp.bfloat16))
        for h in range(QH):
            part = slice(h * tile, (h + 1) * tile)
            acc_ref[h, :, here] = mixed[:, part]
            stat_ref[h : h + 1, here] = top[:, part]
            stat_ref[QH + h : QH + h + 1, here] = total[:, part]


def past_kernel(distances, is_last, lengths_ref, qt_ref, acc_in, stat_in, *refs):
    kv_refs = refs[: len(distances)]
    acc_ref, stat_ref = refs[len(distances) : len(distances) + 2]
    q_rows = qt_ref.shape[2]
    tile = math.gcd(q_rows, 256)
    here = lax.axis_index("ctx")
    odd = here % 2
    own_first = here * q_rows
    first = own_first
    last = own_first
    end = jnp.int32(0)
    for d in range(lengths_ref.shape[0]):
        begin, end = end, end + lengths_ref[d]
        holds = (begin < own_first) & (end > own_first)
        first = jnp.where(holds, begin, first)
        last = jnp.where(holds, end, last)
    live_rows = last - own_first

    def absorb(kv_ref, cut, t):
        cols = slice(t * tile, (t + 1) * tile)
        key = lax.broadcasted_iota(jnp.int32, (q_rows, tile), 0)
        hidden = key < cut
        live = lax.broadcasted_iota(jnp.int32, (1, tile), 1) + t * tile < live_rows
        keys = kv_ref[0]
        values_t = jnp.transpose(kv_ref[1])
        later = dot(keys, qt_ref[0, :, cols])
        for h in range(QH):
            scores = later
            if h + 1 < QH:
                later = dot(keys, qt_ref[h + 1, :, cols])
            scores = jnp.where(hidden, LOW, scores)
            old_top = stat_ref[h : h + 1, cols]
            old_total = stat_ref[QH + h : QH + h + 1, cols]
            top = jnp.maximum(old_top, jnp.max(scores, axis=0, keepdims=True))
            top = jnp.where(live, top, old_top)
            weights = jnp.exp2((scores - top) * EXP2_SCALE)
            total = jnp.sum(weights, axis=0, keepdims=True)
            mixed = dot(values_t, weights.astype(jnp.bfloat16))
            decay = jnp.exp2((old_top - top) * EXP2_SCALE)
            acc_ref[h, :, cols] = acc_ref[h, :, cols] * decay + jnp.where(live, mixed, 0.0)
            stat_ref[h : h + 1, cols] = top
            stat_ref[QH + h : QH + h + 1, cols] = old_total * decay + jnp.where(live, total, 0.0)

    for kv_ref, (even_distance, odd_distance) in zip(kv_refs, distances):
        distance = jnp.where(odd == 1, odd_distance, even_distance)
        shard_first = (here - distance) * q_rows
        for t in range(q_rows // tile):
            seen = (distance > 0) & (live_rows > t * tile) & (first < shard_first + q_rows)
            pl.when(seen)(functools.partial(absorb, kv_ref, first - shard_first, t))

    if is_last:
        out_ref, mass_ref = refs[len(distances) + 2 :]
        for h in range(QH):
            total = stat_ref[QH + h : QH + h + 1, :]
            mixed = acc_ref[h] * (1.0 / total)
            out_ref[:, h * HD : (h + 1) * HD] = jnp.transpose(mixed.astype(jnp.bfloat16))
            mass_ref[h : h + 1, :] = stat_ref[h : h + 1, :] * SCALE + jnp.log(total)


def state_shapes(q_rows):
    return (
        jax.ShapeDtypeStruct((QH, HD, q_rows), jnp.float32),
        jax.ShapeDtypeStruct((2 * QH, q_rows), jnp.float32),
    )


def own_part(lengths, queries, key_rows, values):
    q_rows = queries.shape[0]
    in_smem = pl.BlockSpec(memory_space=pltpu.SMEM)
    in_vmem = pl.BlockSpec(memory_space=pltpu.VMEM)
    qt, *state = pl.pallas_call(
        own_kernel,
        out_shape=(jax.ShapeDtypeStruct((QH, HD, q_rows), jnp.bfloat16),) + state_shapes(q_rows),
        in_specs=[in_smem, in_vmem, in_vmem, in_vmem],
        out_specs=(in_vmem, in_vmem, in_vmem),
        compiler_params=pltpu.CompilerParams(vmem_limit_bytes=VMEM_LIMIT),
        cost_estimate=pl.CostEstimate(
            flops=8 * QH * q_rows * q_rows * HD,
            bytes_accessed=8 * q_rows * QH * HD,
            transcendentals=QH * q_rows * q_rows,
        ),
    )(lengths, queries, key_rows, values)
    return qt, tuple(state)


def past_part(lengths, qt, state, shards, is_last=False):
    q_rows = qt.shape[2]
    distances = [s[0] for s in shards]
    arrays = [s[1] for s in shards]
    in_smem = pl.BlockSpec(memory_space=pltpu.SMEM)
    in_vmem = pl.BlockSpec(memory_space=pltpu.VMEM)
    out_shape = state_shapes(q_rows)
    if is_last:
        out_shape += (
            jax.ShapeDtypeStruct((q_rows, QH * HD), jnp.bfloat16),
            jax.ShapeDtypeStruct((QH, q_rows), jnp.float32),
        )
    outs = pl.pallas_call(
        functools.partial(past_kernel, distances, is_last),
        out_shape=out_shape,
        in_specs=[in_smem] + [in_vmem] * (3 + len(arrays)),
        out_specs=(in_vmem,) * len(out_shape),
        input_output_aliases={2: 0, 3: 1},
        compiler_params=pltpu.CompilerParams(vmem_limit_bytes=VMEM_LIMIT),
        cost_estimate=pl.CostEstimate(
            flops=8 * QH * q_rows * q_rows * HD * len(arrays),
            bytes_accessed=16 * q_rows * QH * HD,
            transcendentals=QH * q_rows * q_rows * len(arrays),
        ),
    )(lengths, qt, *state, *arrays)
    return outs[2:] if is_last else outs


def on_device(lengths, queries, key_rows, values):
    count = lax.axis_size("ctx")
    reach = min(count // 2 + 1, count - 1)
    strides = reach // 2

    def send(value, pairs):
        return lax.ppermute(value, "ctx", pairs)

    own = jnp.stack([key_rows, values])
    moving = send(own, [(i, i + 2) for i in range(count - 2)])
    beside = send(own, [(i, i + 1) for i in range(0, count, 2)])
    qt, state = own_part(lengths, queries, key_rows, values)
    moving, beside, state = lax.optimization_barrier((moving, beside, state))
    side_distances = (0, 1)
    for k in range(1, strides + 1):
        arrived = moving
        shards = [((2 * k, 2 * k), arrived), (side_distances, beside)]
        if k < strides:
            moving = send(arrived, [(i, i + 2) for i in range(2 * k, count - 2)])
        exchange = [(i + 1, i) for i in range(2 * k, count, 2)]
        side_distances = (2 * k - 1, 0)
        if 2 * k + 1 <= reach:
            exchange += [(i, i + 1) for i in range(2 * k, count, 2)]
            side_distances = (2 * k - 1, 2 * k + 1)
        beside = send(arrived, exchange)
        state = past_part(lengths, qt, state, shards)
        if k < strides:
            moving, beside, state = lax.optimization_barrier((moving, beside, state))
    shards = [(side_distances, beside)]
    if reach % 2 == 1:
        own, _ = lax.optimization_barrier((own, moving))
        far = send(own, [(i, i + reach) for i in range(1, count - reach, 2)])
        shards.append(((reach, 0), far))
    return past_part(lengths, qt, state, shards, is_last=True)


def solution(mesh):
    in_specs = (
        P("batch"),
        P(("batch", "ctx"), None),
        P(("batch", "ctx"), None),
        P(("batch", "ctx"), None),
    )
    out_specs = (P(("batch", "ctx"), None), P(None, ("batch", "ctx")))
    return jax.shard_map(
        on_device, mesh=mesh, in_specs=in_specs, out_specs=out_specs, check_vma=False
    )
```

```python
import functools
import math

import jax
import jax.numpy as jnp
from jax import lax
from jax.experimental import pallas as pl
from jax.experimental.pallas import tpu as pltpu
from jax.sharding import PartitionSpec as P

QH = 4
HD = 128
LOW = -1e30
SCALE = 1.0 / math.sqrt(HD)
EXP2_SCALE = SCALE * math.log2(math.e)
VMEM_LIMIT = 32 * 1024 * 1024


def dot(a, b):
    return jnp.dot(a, b, preferred_element_type=jnp.float32)


def own_kernel(lengths_ref, q_ref, k_ref, v_ref, qt_ref, acc_ref, stat_ref):
    q_rows = q_ref.shape[0]
    tile = math.gcd(q_rows, 128)
    own_first = lax.axis_index("ctx") * q_rows
    ends = []
    end = jnp.int32(0)
    for d in range(lengths_ref.shape[0]):
        end = end + lengths_ref[d]
        ends.append(end - own_first)
    values_t = jnp.transpose(v_ref[...])
    for h in range(QH):
        qt_ref[h] = jnp.transpose(q_ref[:, h * HD : (h + 1) * HD])
    for t in range(q_rows // tile):
        keys = (t + 1) * tile
        here = slice(t * tile, (t + 1) * tile)
        row = lax.broadcasted_iota(jnp.int32, (1, tile), 1) + t * tile
        start = jnp.zeros((1, tile), jnp.int32)
        for end in ends:
            start = jnp.where(row >= end, jnp.maximum(start, end), start)
        key = lax.broadcasted_iota(jnp.int32, (keys, tile), 0)
        hidden = (key < start) | (key > row)
        hidden = jnp.concatenate([hidden] * QH, axis=1)
        heads = jnp.concatenate([qt_ref[h, :, here] for h in range(QH)], axis=1)
        scores = jnp.where(hidden, LOW, dot(k_ref[:keys, :], heads))
        top = jnp.max(scores, axis=0, keepdims=True)
        weights = jnp.exp2((scores - top) * EXP2_SCALE)
        total = jnp.sum(weights, axis=0, keepdims=True)
        mixed = dot(values_t[:, :keys], weights.astype(jnp.bfloat16))
        for h in range(QH):
            part = slice(h * tile, (h + 1) * tile)
            acc_ref[h, :, here] = mixed[:, part]
            stat_ref[h : h + 1, here] = top[:, part]
            stat_ref[QH + h : QH + h + 1, here] = total[:, part]


def past_kernel(distances, ones_sum, is_last, lengths_ref, qt_ref, acc_in, stat_in, *refs):
    kv_refs = refs[: len(distances)]
    acc_ref, stat_ref = refs[len(distances) : len(distances) + 2]
    q_rows = qt_ref.shape[2]
    tile = math.gcd(q_rows, 256)
    here = lax.axis_index("ctx")
    odd = here % 2
    own_first = here * q_rows
    first = own_first
    last = own_first
    end = jnp.int32(0)
    for d in range(lengths_ref.shape[0]):
        begin, end = end, end + lengths_ref[d]
        holds = (begin < own_first) & (end > own_first)
        first = jnp.where(holds, begin, first)
        last = jnp.where(holds, end, last)
    live_rows = last - own_first

    def absorb(kv_ref, t, cut=None):
        cols = slice(t * tile, (t + 1) * tile)
        live = lax.broadcasted_iota(jnp.int32, (1, tile), 1) + t * tile < live_rows
        keys = kv_ref[0]
        values_t = jnp.transpose(kv_ref[1])
        if ones_sum:
            values_t = jnp.concatenate([values_t, jnp.ones((16, q_rows), jnp.bfloat16)], axis=0)
        if cut is not None:
            hidden = lax.broadcasted_iota(jnp.int32, (q_rows, tile), 0) < cut
        later = dot(keys, qt_ref[0, :, cols])
        for h in range(QH):
            scores = later
            if h + 1 < QH:
                later = dot(keys, qt_ref[h + 1, :, cols])
            if cut is not None:
                scores = jnp.where(hidden, LOW, scores)
            old_top = stat_ref[h : h + 1, cols]
            old_total = stat_ref[QH + h : QH + h + 1, cols]
            top = jnp.maximum(old_top, jnp.max(scores, axis=0, keepdims=True))
            top = jnp.where(live, top, old_top)
            weights = jnp.exp2((scores - top) * EXP2_SCALE)
            mixed = dot(values_t, weights.astype(jnp.bfloat16))
            if ones_sum:
                total = mixed[HD : HD + 1]
            else:
                total = jnp.sum(weights, axis=0, keepdims=True)
            decay = jnp.exp2((old_top - top) * EXP2_SCALE)
            acc_ref[h, :, cols] = acc_ref[h, :, cols] * decay + jnp.where(live, mixed[:HD], 0.0)
            stat_ref[h : h + 1, cols] = top
            stat_ref[QH + h : QH + h + 1, cols] = old_total * decay + jnp.where(live, total, 0.0)

    for kv_ref, (even_distance, odd_distance) in zip(kv_refs, distances):
        distance = jnp.where(odd == 1, odd_distance, even_distance)
        cut = first - (here - distance) * q_rows
        for t in range(q_rows // tile):
            seen = (distance > 0) & (live_rows > t * tile) & (cut < q_rows)
            pl.when(seen & (cut <= 0))(functools.partial(absorb, kv_ref, t))
            pl.when(seen & (cut > 0))(functools.partial(absorb, kv_ref, t, cut))

    if is_last:
        out_ref, mass_ref = refs[len(distances) + 2 :]
        for h in range(QH):
            total = stat_ref[QH + h : QH + h + 1, :]
            mixed = acc_ref[h] * (1.0 / total)
            out_ref[:, h * HD : (h + 1) * HD] = jnp.transpose(mixed.astype(jnp.bfloat16))
            mass_ref[h : h + 1, :] = stat_ref[h : h + 1, :] * SCALE + jnp.log(total)


def state_shapes(q_rows):
    return (
        jax.ShapeDtypeStruct((QH, HD, q_rows), jnp.float32),
        jax.ShapeDtypeStruct((2 * QH, q_rows), jnp.float32),
    )


def own_part(lengths, queries, key_rows, values):
    q_rows = queries.shape[0]
    in_smem = pl.BlockSpec(memory_space=pltpu.SMEM)
    in_vmem = pl.BlockSpec(memory_space=pltpu.VMEM)
    qt, *state = pl.pallas_call(
        own_kernel,
        out_shape=(jax.ShapeDtypeStruct((QH, HD, q_rows), jnp.bfloat16),) + state_shapes(q_rows),
        in_specs=[in_smem, in_vmem, in_vmem, in_vmem],
        out_specs=(in_vmem, in_vmem, in_vmem),
        compiler_params=pltpu.CompilerParams(vmem_limit_bytes=VMEM_LIMIT),
        cost_estimate=pl.CostEstimate(
            flops=8 * QH * q_rows * q_rows * HD,
            bytes_accessed=8 * q_rows * QH * HD,
            transcendentals=QH * q_rows * q_rows,
        ),
    )(lengths, queries, key_rows, values)
    return qt, tuple(state)


def past_part(lengths, qt, state, shards, ones_sum, is_last=False):
    q_rows = qt.shape[2]
    distances = [s[0] for s in shards]
    arrays = [s[1] for s in shards]
    in_smem = pl.BlockSpec(memory_space=pltpu.SMEM)
    in_vmem = pl.BlockSpec(memory_space=pltpu.VMEM)
    out_shape = state_shapes(q_rows)
    if is_last:
        out_shape += (
            jax.ShapeDtypeStruct((q_rows, QH * HD), jnp.bfloat16),
            jax.ShapeDtypeStruct((QH, q_rows), jnp.float32),
        )
    outs = pl.pallas_call(
        functools.partial(past_kernel, distances, ones_sum, is_last),
        out_shape=out_shape,
        in_specs=[in_smem] + [in_vmem] * (3 + len(arrays)),
        out_specs=(in_vmem,) * len(out_shape),
        input_output_aliases={2: 0, 3: 1},
        compiler_params=pltpu.CompilerParams(vmem_limit_bytes=VMEM_LIMIT),
        cost_estimate=pl.CostEstimate(
            flops=8 * QH * q_rows * q_rows * HD * len(arrays),
            bytes_accessed=16 * q_rows * QH * HD,
            transcendentals=QH * q_rows * q_rows * len(arrays),
        ),
    )(lengths, qt, *state, *arrays)
    return outs[2:] if is_last else outs


def on_device(lengths, queries, key_rows, values):
    count = lax.axis_size("ctx")
    reach = min(count // 2 + 1, count - 1)
    strides = reach // 2

    def send(value, pairs):
        return lax.ppermute(value, "ctx", pairs)

    own = jnp.stack([key_rows, values])
    pairs = [(i, i + 1) for i in range(0, count, 2)]
    if reach % 2 == 1:
        pairs += [(i + 1, i) for i in range(0, count - reach - 1, 2)]
    beside = send(own, pairs)
    moving = send(own, [(i, i + 2) for i in range(count - 2)])
    first_beside = beside
    qt, state = own_part(lengths, queries, key_rows, values)
    beside, moving, state = lax.optimization_barrier((beside, moving, state))
    side_distances = (0, 1)
    for k in range(1, strides + 1):
        arrived = moving
        shards = [((2 * k, 2 * k), arrived), (side_distances, beside)]
        exchange = [(i + 1, i) for i in range(2 * k, count, 2)]
        side_distances = (2 * k - 1, 0)
        if 2 * k + 1 <= reach:
            exchange += [(i, i + 1) for i in range(2 * k, count, 2)]
            side_distances = (2 * k - 1, 2 * k + 1)
        beside = send(arrived, exchange)
        if k < strides:
            moving = send(arrived, [(i, i + 2) for i in range(2 * k, count - 2)])
        state = past_part(lengths, qt, state, shards, k > 1)
        if k < strides:
            beside, moving, state = lax.optimization_barrier((beside, moving, state))
    shards = [(side_distances, beside)]
    if reach % 2 == 1:
        first_beside, _ = lax.optimization_barrier((first_beside, moving))
        far = send(first_beside, [(i, i + reach + 1) for i in range(0, count - reach - 1, 2)])
        shards.insert(0, ((reach, 0), far))
    return past_part(lengths, qt, state, shards, True, is_last=True)


def solution(mesh):
    in_specs = (
        P("batch"),
        P(("batch", "ctx"), None),
        P(("batch", "ctx"), None),
        P(("batch", "ctx"), None),
    )
    out_specs = (P(("batch", "ctx"), None), P(None, ("batch", "ctx")))
    return jax.shard_map(
        on_device, mesh=mesh, in_specs=in_specs, out_specs=out_specs, check_vma=False
    )
```

```python
import functools
import math

import jax
import jax.numpy as jnp
from jax import lax
from jax.experimental import pallas as pl
from jax.experimental.pallas import tpu as pltpu
from jax.sharding import PartitionSpec as P

QH = 4
HD = 128
LOW = -1e30
SCALE = 1.0 / math.sqrt(HD)
EXP2_SCALE = SCALE * math.log2(math.e)
VMEM_LIMIT = 32 * 1024 * 1024
LITTLE = pl.CostEstimate(flops=1024, bytes_accessed=1024, transcendentals=0)


def dot(a, b):
    return jnp.dot(a, b, preferred_element_type=jnp.float32)


def own_kernel(lengths_ref, q_ref, k_ref, v_ref, qt_ref, acc_ref, stat_ref):
    q_rows = q_ref.shape[0]
    tile = math.gcd(q_rows, 128)
    own_first = lax.axis_index("ctx") * q_rows
    ends = []
    end = jnp.int32(0)
    for d in range(lengths_ref.shape[0]):
        end = end + lengths_ref[d]
        ends.append(end - own_first)
    values_t = jnp.transpose(v_ref[...])
    for h in range(QH):
        qt_ref[h] = jnp.transpose(q_ref[:, h * HD : (h + 1) * HD])
    for t in range(q_rows // tile):
        keys = (t + 1) * tile
        here = slice(t * tile, (t + 1) * tile)
        row = lax.broadcasted_iota(jnp.int32, (1, tile), 1) + t * tile
        start = jnp.zeros((1, tile), jnp.int32)
        for end in ends:
            start = jnp.where(row >= end, jnp.maximum(start, end), start)
        key = lax.broadcasted_iota(jnp.int32, (keys, tile), 0)
        hidden = (key < start) | (key > row)
        hidden = jnp.concatenate([hidden] * QH, axis=1)
        heads = jnp.concatenate([qt_ref[h, :, here] for h in range(QH)], axis=1)
        scores = jnp.where(hidden, LOW, dot(k_ref[:keys, :], heads))
        top = jnp.max(scores, axis=0, keepdims=True)
        weights = jnp.exp2((scores - top) * EXP2_SCALE)
        total = jnp.sum(weights, axis=0, keepdims=True)
        mixed = dot(values_t[:, :keys], weights.astype(jnp.bfloat16))
        for h in range(QH):
            part = slice(h * tile, (h + 1) * tile)
            acc_ref[h, :, here] = mixed[:, part]
            stat_ref[h : h + 1, here] = top[:, part]
            stat_ref[QH + h : QH + h + 1, here] = total[:, part]


def past_kernel(distances, ones_sum, is_last, lengths_ref, qt_ref, acc_in, stat_in, *refs):
    kv_refs = refs[: len(distances)]
    acc_ref, stat_ref = refs[len(distances) : len(distances) + 2]
    q_rows = qt_ref.shape[2]
    tile = math.gcd(q_rows, 256)
    here = lax.axis_index("ctx")
    odd = here % 2
    own_first = here * q_rows
    first = own_first
    last = own_first
    end = jnp.int32(0)
    for d in range(lengths_ref.shape[0]):
        begin, end = end, end + lengths_ref[d]
        holds = (begin < own_first) & (end > own_first)
        first = jnp.where(holds, begin, first)
        last = jnp.where(holds, end, last)
    live_rows = last - own_first

    def absorb(kv_ref, t, skipped=0, cut=None):
        cols = slice(t * tile, (t + 1) * tile)
        live = lax.broadcasted_iota(jnp.int32, (1, tile), 1) + t * tile < live_rows
        keys = kv_ref[0, skipped:]
        values_t = jnp.transpose(kv_ref[1, skipped:])
        rows = keys.shape[0]
        if ones_sum:
            values_t = jnp.concatenate([values_t, jnp.ones((16, rows), jnp.bfloat16)], axis=0)
        group = 1 if ones_sum else QH
        width = group * tile
        live = jnp.concatenate([live] * group, axis=1)
        if cut is not None:
            hidden = lax.broadcasted_iota(jnp.int32, (rows, width), 0) + skipped < cut

        def side_by_side(read, g):
            return jnp.concatenate([read(g + h) for h in range(group)], axis=1)

        def product(g):
            return dot(keys, side_by_side(lambda h: qt_ref[h, :, cols], g))

        later = product(0)
        for g in range(0, QH, group):
            scores = later
            if g + group < QH:
                later = product(g + group)
            if cut is not None:
                scores = jnp.where(hidden, LOW, scores)
            old_top = side_by_side(lambda h: stat_ref[h : h + 1, cols], g)
            old_total = side_by_side(lambda h: stat_ref[QH + h : QH + h + 1, cols], g)
            top = jnp.maximum(old_top, jnp.max(scores, axis=0, keepdims=True))
            top = jnp.where(live, top, old_top)
            weights = jnp.exp2((scores - top) * EXP2_SCALE)
            mixed = dot(values_t, weights.astype(jnp.bfloat16))
            if ones_sum:
                total = mixed[HD : HD + 1]
            else:
                total = jnp.sum(weights, axis=0, keepdims=True)
            decay = jnp.exp2((old_top - top) * EXP2_SCALE)
            total = old_total * decay + jnp.where(live, total, 0.0)
            mixed = jnp.where(live, mixed[:HD], 0.0)
            for h in range(group):
                part = slice(h * tile, (h + 1) * tile)
                n = g + h
                acc_ref[n, :, cols] = acc_ref[n, :, cols] * decay[:, part] + mixed[:, part]
                stat_ref[n : n + 1, cols] = top[:, part]
                stat_ref[QH + n : QH + n + 1, cols] = total[:, part]

    half = q_rows // 2
    for kv_ref, (even_distance, odd_distance) in zip(kv_refs, distances):
        distance = jnp.where(odd == 1, odd_distance, even_distance)
        cut = first - (here - distance) * q_rows
        for t in range(q_rows // tile):
            seen = (distance > 0) & (live_rows > t * tile) & (cut < q_rows)
            pl.when(seen & (cut <= 0))(functools.partial(absorb, kv_ref, t))
            pl.when(seen & (cut > 0) & (cut < half))(
                functools.partial(absorb, kv_ref, t, 0, cut)
            )
            pl.when(seen & (cut >= half))(
                functools.partial(absorb, kv_ref, t, half, cut)
            )

    if is_last:
        out_ref, mass_ref = refs[len(distances) + 2 :]
        for h in range(QH):
            total = stat_ref[QH + h : QH + h + 1, :]
            mixed = acc_ref[h] * (1.0 / total)
            out_ref[:, h * HD : (h + 1) * HD] = jnp.transpose(mixed.astype(jnp.bfloat16))
            mass_ref[h : h + 1, :] = stat_ref[h : h + 1, :] * SCALE + jnp.log(total)


def state_shapes(q_rows):
    return (
        jax.ShapeDtypeStruct((QH, HD, q_rows), jnp.float32),
        jax.ShapeDtypeStruct((2 * QH, q_rows), jnp.float32),
    )


def stack_kernel(k_ref, v_ref, out_ref, sem):
    copies = [
        pltpu.make_async_copy(ref, out_ref.at[n], sem.at[n]) for n, ref in enumerate((k_ref, v_ref))
    ]
    for copy in copies:
        copy.start()
    for copy in copies:
        copy.wait()


def stacked(key_rows, values):
    return pl.pallas_call(
        stack_kernel,
        out_shape=jax.ShapeDtypeStruct((2,) + key_rows.shape, key_rows.dtype),
        in_specs=[pl.BlockSpec(memory_space=pltpu.HBM)] * 2,
        out_specs=pl.BlockSpec(memory_space=pltpu.VMEM),
        scratch_shapes=[pltpu.SemaphoreType.DMA((2,))],
    )(key_rows, values)


def own_part(lengths, queries, key_rows, values):
    q_rows = queries.shape[0]
    in_smem = pl.BlockSpec(memory_space=pltpu.SMEM)
    in_vmem = pl.BlockSpec(memory_space=pltpu.VMEM)
    qt, *state = pl.pallas_call(
        own_kernel,
        out_shape=(jax.ShapeDtypeStruct((QH, HD, q_rows), jnp.bfloat16),) + state_shapes(q_rows),
        in_specs=[in_smem, in_vmem, in_vmem, in_vmem],
        out_specs=(in_vmem, in_vmem, in_vmem),
        compiler_params=pltpu.CompilerParams(vmem_limit_bytes=VMEM_LIMIT),
        cost_estimate=LITTLE,
    )(lengths, queries, key_rows, values)
    return qt, tuple(state)


def past_part(lengths, qt, state, shards, ones_sum, is_last=False):
    q_rows = qt.shape[2]
    distances = [s[0] for s in shards]
    arrays = [s[1] for s in shards]
    in_smem = pl.BlockSpec(memory_space=pltpu.SMEM)
    in_vmem = pl.BlockSpec(memory_space=pltpu.VMEM)
    out_shape = state_shapes(q_rows)
    if is_last:
        out_shape += (
            jax.ShapeDtypeStruct((q_rows, QH * HD), jnp.bfloat16),
            jax.ShapeDtypeStruct((QH, q_rows), jnp.float32),
        )
    outs = pl.pallas_call(
        functools.partial(past_kernel, distances, ones_sum, is_last),
        out_shape=out_shape,
        in_specs=[in_smem] + [in_vmem] * (3 + len(arrays)),
        out_specs=(in_vmem,) * len(out_shape),
        input_output_aliases={2: 0, 3: 1},
        compiler_params=pltpu.CompilerParams(vmem_limit_bytes=VMEM_LIMIT),
        cost_estimate=LITTLE,
    )(lengths, qt, *state, *arrays)
    return outs[2:] if is_last else outs


def on_device(lengths, queries, key_rows, values):
    count = lax.axis_size("ctx")
    reach = min(count // 2 + 1, count - 1)
    strides = reach // 2

    def send(value, pairs):
        return lax.ppermute(value, "ctx", pairs)

    own = stacked(key_rows, values)
    moving = send(own, [(i, i + 2) for i in range(count - 2)])
    pairs = [(i, i + 1) for i in range(0, count, 2)]
    if reach % 2 == 1:
        pairs += [(i + 1, i) for i in range(0, count - reach - 1, 2)]
    beside = first_beside = send(own, pairs)
    qt, state = own_part(lengths, queries, key_rows, values)
    moving, state = lax.optimization_barrier((moving, state))
    side_distances = (0, 1)
    for k in range(1, strides + 1):
        arrived = moving
        if k < strides:
            moving = send(arrived, [(i, i + 2) for i in range(2 * k, count - 2)])
        shards = [((2 * k, 2 * k), arrived), (side_distances, beside)]
        exchange = [(i + 1, i) for i in range(2 * k, count, 2)]
        side_distances = (2 * k - 1, 0)
        if 2 * k + 1 <= reach:
            exchange += [(i, i + 1) for i in range(2 * k, count, 2)]
            side_distances = (2 * k - 1, 2 * k + 1)
        beside = send(arrived, exchange)
        state = past_part(lengths, qt, state, shards, k > 1)
        if k < strides:
            moving, state = lax.optimization_barrier((moving, state))
    shards = [(side_distances, beside)]
    if reach % 2 == 1:
        first_beside, _ = lax.optimization_barrier((first_beside, moving))
        far = send(first_beside, [(i, i + reach + 1) for i in range(0, count - reach - 1, 2)])
        shards.insert(0, ((reach, 0), far))
    return past_part(lengths, qt, state, shards, True, is_last=True)


def solution(mesh):
    in_specs = (
        P("batch"),
        P(("batch", "ctx"), None),
        P(("batch", "ctx"), None),
        P(("batch", "ctx"), None),
    )
    out_specs = (P(("batch", "ctx"), None), P(None, ("batch", "ctx")))
    return jax.shard_map(
        on_device, mesh=mesh, in_specs=in_specs, out_specs=out_specs, check_vma=False
    )
```

```python
import functools
import math

import jax
import jax.numpy as jnp
from jax import lax
from jax.experimental import pallas as pl
from jax.experimental.pallas import tpu as pltpu
from jax.sharding import PartitionSpec as P

QH = 4
HD = 128
LOW = -1e30
SCALE = 1.0 / math.sqrt(HD)
EXP2_SCALE = SCALE * math.log2(math.e)
VMEM_LIMIT = 32 * 1024 * 1024
LITTLE = pl.CostEstimate(flops=1024, bytes_accessed=1024, transcendentals=0)


def dot(a, b):
    return jnp.dot(a, b, preferred_element_type=jnp.float32)


def scores_of(heads, keys):
    return lax.dot_general(
        heads, keys, (((1,), (1,)), ((), ())), preferred_element_type=jnp.float32
    )


def lane_parts(tile, combine):
    parts = [tile[:, c : c + HD] for c in range(0, tile.shape[1], HD)]
    return functools.reduce(combine, parts)


def beside_ones(rows):
    return jnp.concatenate([rows, jnp.ones_like(rows)], axis=1)


def over_heads(read):
    return jnp.concatenate([read(h) for h in range(QH)], axis=0)


def heads_of(q_ref, rows_at):
    return over_heads(lambda h: q_ref[rows_at, h * HD : (h + 1) * HD])


def row_top(scores):
    top = jnp.max(lane_parts(scores, jnp.maximum), axis=1, keepdims=True)
    return jnp.broadcast_to(top, (scores.shape[0], HD))


def weights_of(scores, top):
    wide = jnp.concatenate([top] * (scores.shape[1] // HD), axis=1)
    return jnp.exp2((scores - wide) * EXP2_SCALE).astype(jnp.bfloat16)


def own_kernel(lengths_ref, q_ref, kv_ref, acc_ref, top_ref, total_ref):
    q_rows = q_ref.shape[0]
    tile = math.gcd(q_rows, 128)
    own_first = lax.axis_index("ctx") * q_rows
    ends = []
    end = jnp.int32(0)
    for d in range(lengths_ref.shape[0]):
        end = end + lengths_ref[d]
        ends.append(end - own_first)
    for t in range(q_rows // tile):
        keys = (t + 1) * tile
        here = slice(t * tile, (t + 1) * tile)
        row = lax.broadcasted_iota(jnp.int32, (tile, HD), 0) + t * tile
        start = jnp.zeros((tile, HD), jnp.int32)
        for end in ends:
            start = jnp.where(row >= end, jnp.maximum(start, end), start)
        start = jnp.concatenate([start] * (keys // HD), axis=1)
        row = lax.broadcasted_iota(jnp.int32, (tile, keys), 0) + t * tile
        key = lax.broadcasted_iota(jnp.int32, (tile, keys), 1)
        hidden = (key < start) | (key > row)
        scores = scores_of(heads_of(q_ref, here), kv_ref[0, :keys])
        scores = jnp.where(over_heads(lambda h: hidden), LOW, scores)
        top = row_top(scores)
        mixed = dot(weights_of(scores, top), beside_ones(kv_ref[1, :keys]))
        for h in range(QH):
            part = slice(h * tile, (h + 1) * tile)
            acc_ref[h, here, :] = mixed[part, :HD]
            top_ref[h, here, :] = top[part]
            total_ref[h, here, :] = mixed[part, HD:]


def past_kernel(distances, is_last, lengths_ref, q_ref, acc_in, top_in, total_in, *refs):
    kv_refs = refs[: len(distances)]
    acc_ref, top_ref, total_ref = refs[len(distances) : len(distances) + 3]
    q_rows = q_ref.shape[0]
    tile = math.gcd(q_rows, 256)
    half = q_rows // 2
    here = lax.axis_index("ctx")
    odd = here % 2
    own_first = here * q_rows
    first = own_first
    last = own_first
    end = jnp.int32(0)
    for d in range(lengths_ref.shape[0]):
        begin, end = end, end + lengths_ref[d]
        holds = (begin < own_first) & (end > own_first)
        first = jnp.where(holds, begin, first)
        last = jnp.where(holds, end, last)
    live_rows = jnp.minimum(last - own_first, q_rows)

    def absorb(kv_ref, skipped=0, cut=None):
        def absorb_tile(t, _):
            rows_at = pl.ds(pl.multiple_of(t * tile, tile), tile)
            row = lax.broadcasted_iota(jnp.int32, (tile, HD), 0) + t * tile
            live = over_heads(lambda h: row < live_rows)
            scores = scores_of(heads_of(q_ref, rows_at), kv_ref[0, skipped:])
            if cut is not None:
                key = lax.broadcasted_iota(jnp.int32, scores.shape, 1) + skipped
                scores = jnp.where(key < cut, LOW, scores)
            old_top = over_heads(lambda h: top_ref[h, rows_at, :])
            top = jnp.where(live, jnp.maximum(old_top, row_top(scores)), old_top)
            mixed = dot(weights_of(scores, top), beside_ones(kv_ref[1, skipped:]))
            decay = jnp.exp2((old_top - top) * EXP2_SCALE)
            added = jnp.where(live, mixed[:, :HD], 0.0)
            counted = jnp.where(live, mixed[:, HD:], 0.0)
            for h in range(QH):
                part = slice(h * tile, (h + 1) * tile)
                acc_ref[h, rows_at, :] = acc_ref[h, rows_at, :] * decay[part] + added[part]
                total_ref[h, rows_at, :] = total_ref[h, rows_at, :] * decay[part] + counted[part]
                top_ref[h, rows_at, :] = top[part]
            return 0

        lax.fori_loop(0, (live_rows + tile - 1) // tile, absorb_tile, 0)

    for kv_ref, (even_distance, odd_distance) in zip(kv_refs, distances):
        distance = jnp.where(odd == 1, odd_distance, even_distance)
        cut = first - (here - distance) * q_rows
        seen = (distance > 0) & (live_rows > 0) & (cut < q_rows)
        pl.when(seen & (cut <= 0))(functools.partial(absorb, kv_ref))
        pl.when(seen & (cut > 0) & (cut < half))(functools.partial(absorb, kv_ref, 0, cut))
        pl.when(seen & (cut >= half))(functools.partial(absorb, kv_ref, half, cut))

    if is_last:
        out_ref, mass_ref = refs[len(distances) + 3 :]
        chunk = math.gcd(q_rows, HD)
        lane = lax.broadcasted_iota(jnp.int32, (chunk, HD), 1)
        for c in range(0, q_rows, chunk):
            rows_at = slice(c, c + chunk)
            packed = jnp.zeros((chunk, HD), jnp.float32)
            for h in range(QH):
                total = total_ref[h, rows_at, :]
                mixed = acc_ref[h, rows_at, :] / total
                out_ref[rows_at, h * HD : (h + 1) * HD] = mixed.astype(jnp.bfloat16)
                mass = top_ref[h, rows_at, :] * SCALE + jnp.log(total)
                packed = jnp.where(lane == h, mass, packed)
            mass_ref[:, rows_at] = jnp.transpose(packed)[:QH, :]


def state_shapes(q_rows):
    return (jax.ShapeDtypeStruct((QH, q_rows, HD), jnp.float32),) * 3


def own_part(lengths, queries, own):
    in_smem = pl.BlockSpec(memory_space=pltpu.SMEM)
    in_vmem = pl.BlockSpec(memory_space=pltpu.VMEM)
    return pl.pallas_call(
        own_kernel,
        out_shape=state_shapes(queries.shape[0]),
        in_specs=[in_smem, in_vmem, in_vmem],
        out_specs=(in_vmem,) * 3,
        compiler_params=pltpu.CompilerParams(vmem_limit_bytes=VMEM_LIMIT),
        cost_estimate=LITTLE,
    )(lengths, queries, own)


def past_part(lengths, queries, state, shards, is_last=False):
    q_rows = queries.shape[0]
    distances = [s[0] for s in shards]
    arrays = [s[1] for s in shards]
    in_smem = pl.BlockSpec(memory_space=pltpu.SMEM)
    in_vmem = pl.BlockSpec(memory_space=pltpu.VMEM)
    out_shape = state_shapes(q_rows)
    if is_last:
        out_shape += (
            jax.ShapeDtypeStruct((q_rows, QH * HD), jnp.bfloat16),
            jax.ShapeDtypeStruct((QH, q_rows), jnp.float32),
        )
    outs = pl.pallas_call(
        functools.partial(past_kernel, distances, is_last),
        out_shape=out_shape,
        in_specs=[in_smem] + [in_vmem] * (4 + len(arrays)),
        out_specs=(in_vmem,) * len(out_shape),
        input_output_aliases={2: 0, 3: 1, 4: 2},
        compiler_params=pltpu.CompilerParams(vmem_limit_bytes=VMEM_LIMIT),
        cost_estimate=LITTLE,
    )(lengths, queries, *state, *arrays)
    return outs[3:] if is_last else outs


def on_device(lengths, queries, key_rows, values):
    count = lax.axis_size("ctx")
    reach = min(count // 2 + 1, count - 1)
    strides = reach // 2

    def send(value, pairs):
        return lax.ppermute(value, "ctx", pairs)

    own = jnp.stack([key_rows, values])
    moving = send(own, [(i, i + 2) for i in range(count - 2)])
    pairs = [(i, i + 1) for i in range(0, count, 2)]
    if reach % 2 == 1:
        pairs += [(i + 1, i) for i in range(0, count - reach - 1, 2)]
    beside = first_beside = send(own, pairs)
    state = own_part(lengths, queries, own)
    moving, *state = lax.optimization_barrier((moving, *state))
    side_distances = (0, 1)
    for k in range(1, strides + 1):
        arrived = moving
        if k < strides:
            moving = send(arrived, [(i, i + 2) for i in range(2 * k, count - 2)])
        shards = [((2 * k, 2 * k), arrived), (side_distances, beside)]
        exchange = [(i + 1, i) for i in range(2 * k, count, 2)]
        side_distances = (2 * k - 1, 0)
        if 2 * k + 1 <= reach:
            exchange += [(i, i + 1) for i in range(2 * k, count, 2)]
            side_distances = (2 * k - 1, 2 * k + 1)
        beside = send(arrived, exchange)
        state = past_part(lengths, queries, state, shards)
        if k == strides - 1 and reach % 2 == 1:
            first_beside, *state = lax.optimization_barrier((first_beside, *state))
            far = send(first_beside, [(i, i + reach + 1) for i in range(0, count - reach - 1, 2)])
        if k < strides:
            moving, *state = lax.optimization_barrier((moving, *state))
    shards = [(side_distances, beside)]
    if reach % 2 == 1:
        shards.insert(0, ((reach, 0), far))
    return past_part(lengths, queries, state, shards, is_last=True)


def solution(mesh):
    in_specs = (
        P("batch"),
        P(("batch", "ctx"), None),
        P(("batch", "ctx"), None),
        P(("batch", "ctx"), None),
    )
    out_specs = (P(("batch", "ctx"), None), P(None, ("batch", "ctx")))
    return jax.shard_map(
        on_device, mesh=mesh, in_specs=in_specs, out_specs=out_specs, check_vma=False
    )
```

```python
import functools
import math

import jax
import jax.numpy as jnp
from jax import lax
from jax.experimental import pallas as pl
from jax.experimental.pallas import tpu as pltpu
from jax.sharding import PartitionSpec as P

QH = 4
HD = 128
LOW = -1e30
SCALE = 1.0 / math.sqrt(HD)
EXP2_SCALE = SCALE * math.log2(math.e)
VMEM_LIMIT = 32 * 1024 * 1024
LITTLE = pl.CostEstimate(flops=1024, bytes_accessed=1024, transcendentals=0)


def dot(a, b):
    return jnp.dot(a, b, preferred_element_type=jnp.float32)


def own_kernel(lengths_ref, q_ref, kv_ref, qt_ref, acc_ref, stat_ref):
    q_rows = q_ref.shape[0]
    tile = math.gcd(q_rows, 128)
    own_first = lax.axis_index("ctx") * q_rows
    ends = []
    end = jnp.int32(0)
    for d in range(lengths_ref.shape[0]):
        end = end + lengths_ref[d]
        ends.append(end - own_first)
    values_t = jnp.transpose(kv_ref[1])
    for h in range(QH):
        qt_ref[h] = jnp.transpose(q_ref[:, h * HD : (h + 1) * HD])
    for t in range(q_rows // tile):
        keys = (t + 1) * tile
        here = slice(t * tile, (t + 1) * tile)
        row = lax.broadcasted_iota(jnp.int32, (1, tile), 1) + t * tile
        start = jnp.zeros((1, tile), jnp.int32)
        for end in ends:
            start = jnp.where(row >= end, jnp.maximum(start, end), start)
        key = lax.broadcasted_iota(jnp.int32, (keys, tile), 0)
        hidden = (key < start) | (key > row)
        hidden = jnp.concatenate([hidden] * QH, axis=1)
        heads = jnp.concatenate([qt_ref[h, :, here] for h in range(QH)], axis=1)
        scores = jnp.where(hidden, LOW, dot(kv_ref[0, :keys, :], heads))
        top = jnp.max(scores, axis=0, keepdims=True)
        weights = jnp.exp2((scores - top) * EXP2_SCALE)
        total = jnp.sum(weights, axis=0, keepdims=True)
        mixed = dot(values_t[:, :keys], weights.astype(jnp.bfloat16))
        for h in range(QH):
            part = slice(h * tile, (h + 1) * tile)
            acc_ref[h, :, here] = mixed[:, part]
            stat_ref[h : h + 1, here] = top[:, part]
            stat_ref[QH + h : QH + h + 1, here] = total[:, part]


def past_kernel(distances, is_last, lengths_ref, qt_ref, acc_in, stat_in, *refs):
    kv_refs = refs[: len(distances)]
    acc_ref, stat_ref = refs[len(distances) : len(distances) + 2]
    q_rows = qt_ref.shape[2]
    tile = math.gcd(q_rows, 256)
    half = q_rows // 2
    here = lax.axis_index("ctx")
    odd = here % 2
    own_first = here * q_rows
    first = own_first
    last = own_first
    end = jnp.int32(0)
    for d in range(lengths_ref.shape[0]):
        begin, end = end, end + lengths_ref[d]
        holds = (begin < own_first) & (end > own_first)
        first = jnp.where(holds, begin, first)
        last = jnp.where(holds, end, last)
    live_rows = last - own_first

    def side_by_side(read):
        return jnp.concatenate([read(h) for h in range(QH)], axis=1)

    def absorb(kv_ref, t, skipped=0, cut=None):
        cols = slice(t * tile, (t + 1) * tile)
        live = lax.broadcasted_iota(jnp.int32, (1, tile), 1) + t * tile < live_rows
        live = side_by_side(lambda h: live)
        scores = dot(kv_ref[0, skipped:], side_by_side(lambda h: qt_ref[h, :, cols]))
        if cut is not None:
            hidden = lax.broadcasted_iota(jnp.int32, scores.shape, 0) + skipped < cut
            scores = jnp.where(hidden, LOW, scores)
        old_top = side_by_side(lambda h: stat_ref[h : h + 1, cols])
        old_total = side_by_side(lambda h: stat_ref[QH + h : QH + h + 1, cols])
        top = jnp.maximum(old_top, jnp.max(scores, axis=0, keepdims=True))
        top = jnp.where(live, top, old_top)
        weights = jnp.exp2((scores - top) * EXP2_SCALE)
        total = jnp.sum(weights, axis=0, keepdims=True)
        mixed = dot(jnp.transpose(kv_ref[1, skipped:]), weights.astype(jnp.bfloat16))
        decay = jnp.exp2((old_top - top) * EXP2_SCALE)
        total = old_total * decay + jnp.where(live, total, 0.0)
        mixed = jnp.where(live, mixed, 0.0)
        for h in range(QH):
            part = slice(h * tile, (h + 1) * tile)
            acc_ref[h, :, cols] = acc_ref[h, :, cols] * decay[:, part] + mixed[:, part]
            stat_ref[h : h + 1, cols] = top[:, part]
            stat_ref[QH + h : QH + h + 1, cols] = total[:, part]

    for kv_ref, (even_distance, odd_distance) in zip(kv_refs, distances):
        distance = jnp.where(odd == 1, odd_distance, even_distance)
        cut = first - (here - distance) * q_rows
        for t in range(q_rows // tile):
            seen = (distance > 0) & (live_rows > t * tile) & (cut < q_rows)
            pl.when(seen & (cut <= 0))(functools.partial(absorb, kv_ref, t))
            pl.when(seen & (cut > 0) & (cut < half))(
                functools.partial(absorb, kv_ref, t, 0, cut)
            )
            pl.when(seen & (cut >= half))(functools.partial(absorb, kv_ref, t, half, cut))

    if is_last:
        out_hbm, mass_ref, out_ref, sem = refs[len(distances) + 2 :]
        copies = []
        for t in range(q_rows // tile):
            rows_at = slice(t * tile, (t + 1) * tile)
            for h in range(QH):
                share = 1.0 / stat_ref[QH + h : QH + h + 1, rows_at]
                mixed = (acc_ref[h, :, rows_at] * share).astype(jnp.bfloat16)
                out_ref[rows_at, h * HD : (h + 1) * HD] = jnp.transpose(mixed)
            copy = pltpu.make_async_copy(
                out_ref.at[pl.ds(t * tile, tile), :],
                out_hbm.at[pl.ds(t * tile, tile), :],
                sem.at[t],
            )
            copy.start()
            copies.append(copy)
        mass_ref[...] = stat_ref[:QH, :] * SCALE + jnp.log(stat_ref[QH:, :])
        for copy in copies:
            copy.wait()


def state_shapes(q_rows):
    return (
        jax.ShapeDtypeStruct((QH, HD, q_rows), jnp.float32),
        jax.ShapeDtypeStruct((2 * QH, q_rows), jnp.float32),
    )


def own_part(lengths, queries, own):
    q_rows = queries.shape[0]
    in_smem = pl.BlockSpec(memory_space=pltpu.SMEM)
    in_vmem = pl.BlockSpec(memory_space=pltpu.VMEM)
    qt, *state = pl.pallas_call(
        own_kernel,
        out_shape=(jax.ShapeDtypeStruct((QH, HD, q_rows), jnp.bfloat16),) + state_shapes(q_rows),
        in_specs=[in_smem, in_vmem, in_vmem],
        out_specs=(in_vmem, in_vmem, in_vmem),
        compiler_params=pltpu.CompilerParams(vmem_limit_bytes=VMEM_LIMIT),
        cost_estimate=LITTLE,
    )(lengths, queries, own)
    return qt, state


def past_part(lengths, qt, state, shards, is_last=False):
    q_rows = qt.shape[2]
    distances = [s[0] for s in shards]
    arrays = [s[1] for s in shards]
    in_smem = pl.BlockSpec(memory_space=pltpu.SMEM)
    in_vmem = pl.BlockSpec(memory_space=pltpu.VMEM)
    out_shape = state_shapes(q_rows)
    out_specs = (in_vmem, in_vmem)
    scratch = []
    if is_last:
        out = jax.ShapeDtypeStruct((q_rows, QH * HD), jnp.bfloat16)
        out_shape += (out, jax.ShapeDtypeStruct((QH, q_rows), jnp.float32))
        out_specs += (pl.BlockSpec(memory_space=pl.ANY), in_vmem)
        tiles = q_rows // math.gcd(q_rows, 256)
        scratch = [pltpu.VMEM(out.shape, out.dtype), pltpu.SemaphoreType.DMA((tiles,))]
    outs = pl.pallas_call(
        functools.partial(past_kernel, distances, is_last),
        out_shape=out_shape,
        in_specs=[in_smem] + [in_vmem] * (3 + len(arrays)),
        out_specs=out_specs,
        scratch_shapes=scratch,
        input_output_aliases={2: 0, 3: 1},
        compiler_params=pltpu.CompilerParams(vmem_limit_bytes=VMEM_LIMIT),
        cost_estimate=LITTLE,
    )(lengths, qt, *state, *arrays)
    return outs[2:] if is_last else outs


def on_device(lengths, queries, key_rows, values):
    count = lax.axis_size("ctx")
    reach = min(count // 2 + 1, count - 1)
    strides = reach // 2

    def send(value, pairs):
        return lax.ppermute(value, "ctx", pairs)

    own = jnp.stack([key_rows, values])
    moving = send(own, [(i, i + 2) for i in range(count - 2)])
    qt, state = own_part(lengths, queries, own)
    own, *state = lax.optimization_barrier((own, *state))
    pairs = [(i, i + 1) for i in range(0, count, 2)]
    if reach % 2 == 1:
        pairs += [(i + 1, i) for i in range(0, count - reach - 1, 2)]
    beside = first_beside = send(own, pairs)
    moving, *state = lax.optimization_barrier((moving, *state))
    side = [((0, 1), beside)]
    for k in range(1, strides + 1):
        arrived = moving
        if k < strides:
            moving = send(arrived, [(i, i + 2) for i in range(2 * k, count - 2)])
        exchange = [(i + 1, i) for i in range(2 * k, count, 2)]
        distances = (2 * k - 1, 0)
        if 2 * k + 1 <= reach:
            exchange += [(i, i + 1) for i in range(2 * k, count, 2)]
            distances = (2 * k - 1, 2 * k + 1)
        shards = [((2 * k, 2 * k), arrived)] + (side if k > 1 else [])
        side = (side if k == 1 else []) + [(distances, send(arrived, exchange))]
        state = past_part(lengths, qt, state, shards)
        if k == strides - 1 and reach % 2 == 1:
            first_beside, *state = lax.optimization_barrier((first_beside, *state))
            far = send(first_beside, [(i, i + reach + 1) for i in range(0, count - reach - 1, 2)])
        if k < strides:
            moving, *state = lax.optimization_barrier((moving, *state))
    if reach % 2 == 1:
        side.insert(0, ((reach, 0), far))
    return past_part(lengths, qt, state, side, is_last=True)


def solution(mesh):
    in_specs = (
        P("batch"),
        P(("batch", "ctx"), None),
        P(("batch", "ctx"), None),
        P(("batch", "ctx"), None),
    )
    out_specs = (P(("batch", "ctx"), None), P(None, ("batch", "ctx")))
    return jax.shard_map(
        on_device, mesh=mesh, in_specs=in_specs, out_specs=out_specs, check_vma=False
    )
```

```python
import functools
import math

import jax
import jax.numpy as jnp
from jax import lax
from jax.experimental import pallas as pl
from jax.experimental.pallas import tpu as pltpu
from jax.sharding import PartitionSpec as P

QH = 4
HD = 128
LOW = -1e30
SCALE = 1.0 / math.sqrt(HD)
EXP2_SCALE = SCALE * math.log2(math.e)
VMEM_LIMIT = 32 * 1024 * 1024
LITTLE = pl.CostEstimate(flops=1024, bytes_accessed=1024, transcendentals=0)


def dot(a, b):
    return jnp.dot(a, b, preferred_element_type=jnp.float32)


def own_kernel(lengths_ref, q_ref, kv_ref, qt_ref, acc_ref, stat_ref):
    q_rows = q_ref.shape[0]
    tile = math.gcd(q_rows, 128)
    own_first = lax.axis_index("ctx") * q_rows
    ends = []
    end = jnp.int32(0)
    for d in range(lengths_ref.shape[0]):
        end = end + lengths_ref[d]
        ends.append(end - own_first)
    values_t = jnp.transpose(kv_ref[1])
    for h in range(QH):
        qt_ref[h] = jnp.transpose(q_ref[:, h * HD : (h + 1) * HD])
    for t in range(q_rows // tile):
        keys = (t + 1) * tile
        here = slice(t * tile, (t + 1) * tile)
        row = lax.broadcasted_iota(jnp.int32, (1, tile), 1) + t * tile
        start = jnp.zeros((1, tile), jnp.int32)
        for end in ends:
            start = jnp.where(row >= end, jnp.maximum(start, end), start)
        key = lax.broadcasted_iota(jnp.int32, (keys, tile), 0)
        hidden = (key < start) | (key > row)
        hidden = jnp.concatenate([hidden] * QH, axis=1)
        heads = jnp.concatenate([qt_ref[h, :, here] for h in range(QH)], axis=1)
        scores = jnp.where(hidden, LOW, dot(kv_ref[0, :keys, :], heads))
        top = jnp.max(scores, axis=0, keepdims=True)
        weights = jnp.exp2((scores - top) * EXP2_SCALE)
        total = jnp.sum(weights, axis=0, keepdims=True)
        mixed = dot(values_t[:, :keys], weights.astype(jnp.bfloat16))
        for h in range(QH):
            part = slice(h * tile, (h + 1) * tile)
            acc_ref[h, :, here] = mixed[:, part]
            stat_ref[h : h + 1, here] = top[:, part]
            stat_ref[QH + h : QH + h + 1, here] = total[:, part]


def past_kernel(distances, is_last, lengths_ref, qt_ref, acc_in, stat_in, *refs):
    kv_refs = refs[: len(distances)]
    acc_ref, stat_ref = refs[len(distances) : len(distances) + 2]
    q_rows = qt_ref.shape[2]
    tile = math.gcd(q_rows, 256)
    half = q_rows // 2
    here = lax.axis_index("ctx")
    odd = here % 2
    own_first = here * q_rows
    first = own_first
    last = own_first
    end = jnp.int32(0)
    for d in range(lengths_ref.shape[0]):
        begin, end = end, end + lengths_ref[d]
        holds = (begin < own_first) & (end > own_first)
        first = jnp.where(holds, begin, first)
        last = jnp.where(holds, end, last)
    live_rows = last - own_first

    def side_by_side(read):
        return jnp.concatenate([read(h) for h in range(QH)], axis=1)

    def absorb(kv_ref, t, skipped=0, cut=None):
        cols = slice(t * tile, (t + 1) * tile)
        live = lax.broadcasted_iota(jnp.int32, (1, tile), 1) + t * tile < live_rows
        live = side_by_side(lambda h: live)
        scores = dot(kv_ref[0, skipped:], side_by_side(lambda h: qt_ref[h, :, cols]))
        if cut is not None:
            hidden = lax.broadcasted_iota(jnp.int32, scores.shape, 0) + skipped < cut
            scores = jnp.where(hidden, LOW, scores)
        old_top = side_by_side(lambda h: stat_ref[h : h + 1, cols])
        old_total = side_by_side(lambda h: stat_ref[QH + h : QH + h + 1, cols])
        top = jnp.maximum(old_top, jnp.max(scores, axis=0, keepdims=True))
        top = jnp.where(live, top, old_top)
        weights = jnp.exp2((scores - top) * EXP2_SCALE)
        total = jnp.sum(weights, axis=0, keepdims=True)
        mixed = dot(jnp.transpose(kv_ref[1, skipped:]), weights.astype(jnp.bfloat16))
        decay = jnp.exp2((old_top - top) * EXP2_SCALE)
        total = old_total * decay + jnp.where(live, total, 0.0)
        mixed = jnp.where(live, mixed, 0.0)
        for h in range(QH):
            part = slice(h * tile, (h + 1) * tile)
            acc_ref[h, :, cols] = acc_ref[h, :, cols] * decay[:, part] + mixed[:, part]
            stat_ref[h : h + 1, cols] = top[:, part]
            stat_ref[QH + h : QH + h + 1, cols] = total[:, part]

    for kv_ref, (even_distance, odd_distance) in zip(kv_refs, distances):
        distance = jnp.where(odd == 1, odd_distance, even_distance)
        cut = first - (here - distance) * q_rows
        for t in range(q_rows // tile):
            seen = (distance > 0) & (live_rows > t * tile) & (cut < q_rows)
            pl.when(seen & (cut <= 0))(functools.partial(absorb, kv_ref, t))
            pl.when(seen & (cut > 0) & (cut < half))(
                functools.partial(absorb, kv_ref, t, 0, cut)
            )
            pl.when(seen & (cut >= half))(functools.partial(absorb, kv_ref, t, half, cut))

    if is_last:
        out_ref, mass_ref = refs[len(distances) + 2 :]
        for h in range(QH):
            mixed = acc_ref[h] * (1.0 / stat_ref[QH + h : QH + h + 1, :])
            out_ref[:, h * HD : (h + 1) * HD] = jnp.transpose(mixed.astype(jnp.bfloat16))
        mass_ref[...] = stat_ref[:QH, :] * SCALE + jnp.log(stat_ref[QH:, :])


def state_shapes(q_rows):
    return (
        jax.ShapeDtypeStruct((QH, HD, q_rows), jnp.float32),
        jax.ShapeDtypeStruct((2 * QH, q_rows), jnp.float32),
    )


def own_part(lengths, queries, own):
    q_rows = queries.shape[0]
    in_smem = pl.BlockSpec(memory_space=pltpu.SMEM)
    in_vmem = pl.BlockSpec(memory_space=pltpu.VMEM)
    qt, *state = pl.pallas_call(
        own_kernel,
        out_shape=(jax.ShapeDtypeStruct((QH, HD, q_rows), jnp.bfloat16),) + state_shapes(q_rows),
        in_specs=[in_smem, in_vmem, in_vmem],
        out_specs=(in_vmem, in_vmem, in_vmem),
        compiler_params=pltpu.CompilerParams(vmem_limit_bytes=VMEM_LIMIT),
        cost_estimate=LITTLE,
    )(lengths, queries, own)
    return qt, state


def past_part(lengths, qt, state, shards, is_last=False):
    q_rows = qt.shape[2]
    distances = [s[0] for s in shards]
    arrays = [s[1] for s in shards]
    in_smem = pl.BlockSpec(memory_space=pltpu.SMEM)
    in_vmem = pl.BlockSpec(memory_space=pltpu.VMEM)
    out_shape = state_shapes(q_rows)
    if is_last:
        out_shape += (
            jax.ShapeDtypeStruct((q_rows, QH * HD), jnp.bfloat16),
            jax.ShapeDtypeStruct((QH, q_rows), jnp.float32),
        )
    outs = pl.pallas_call(
        functools.partial(past_kernel, distances, is_last),
        out_shape=out_shape,
        in_specs=[in_smem] + [in_vmem] * (3 + len(arrays)),
        out_specs=(in_vmem,) * len(out_shape),
        input_output_aliases={2: 0, 3: 1},
        compiler_params=pltpu.CompilerParams(vmem_limit_bytes=VMEM_LIMIT),
        cost_estimate=LITTLE,
    )(lengths, qt, *state, *arrays)
    return outs[2:] if is_last else outs


def on_device(lengths, queries, key_rows, values):
    count = lax.axis_size("ctx")
    reach = min(count // 2 + 1, count - 1)
    strides = reach // 2

    def send(value, pairs):
        return lax.ppermute(value, "ctx", pairs)

    own = jnp.stack([key_rows, values])
    moving = send(own, [(i, i + 2) for i in range(count - 2)])
    qt, state = own_part(lengths, queries, own)
    own, *state = lax.optimization_barrier((own, *state))
    beside = send(own, [(i, i + 1) for i in range(0, count, 2)])
    side = [((0, 1), beside)]
    if reach % 2 == 1:
        far = send(own, [(i, i + reach) for i in range(1, count - reach, 2)])
        side.append(((reach, 0), far))
    moving, *state = lax.optimization_barrier((moving, *state))
    for k in range(1, strides + 1):
        arrived = moving
        shards = [((2 * k, 2 * k), arrived)] + side
        if k < strides:
            moving = send(arrived, [(i, i + 2) for i in range(2 * k, count - 2)])
            exchange = [(i + 1, i) for i in range(2 * k, count, 2)]
            exchange += [(i, i + 1) for i in range(2 * k, count, 2)]
            side = [((2 * k - 1, 2 * k + 1), send(arrived, exchange))]
        if k == strides - 1:
            across = [(i, i + 1) for i in range(2 * k + 1, count - 1, 2)]
            across_distances = (2 * k + 1, 0)
            if 2 * k + 3 <= reach:
                across += [(i, i + 3) for i in range(2 * k, count - 3, 2)]
                across_distances = (2 * k + 1, 2 * k + 3)
            late = [(across_distances, send(arrived, across))]
        state = past_part(lengths, qt, state, shards)
        if k < strides:
            moving, *state = lax.optimization_barrier((moving, *state))
    return past_part(lengths, qt, state, late, is_last=True)


def solution(mesh):
    in_specs = (
        P("batch"),
        P(("batch", "ctx"), None),
        P(("batch", "ctx"), None),
        P(("batch", "ctx"), None),
    )
    out_specs = (P(("batch", "ctx"), None), P(None, ("batch", "ctx")))
    return jax.shard_map(
        on_device, mesh=mesh, in_specs=in_specs, out_specs=out_specs, check_vma=False
    )
```

```python
import functools
import math

import jax
import jax.numpy as jnp
from jax import lax
from jax.experimental import pallas as pl
from jax.experimental.pallas import tpu as pltpu
from jax.sharding import PartitionSpec as P

QH = 4
HD = 128
LOW = -1e30
SCALE = 1.0 / math.sqrt(HD)
EXP2_SCALE = SCALE * math.log2(math.e)
VMEM_LIMIT = 32 * 1024 * 1024
LITTLE = pl.CostEstimate(flops=1024, bytes_accessed=1024, transcendentals=0)


def dot(a, b):
    return jnp.dot(a, b, preferred_element_type=jnp.float32)


def own_kernel(lengths_ref, q_ref, kv_ref, qt_ref, acc_ref, stat_ref):
    q_rows = q_ref.shape[0]
    tile = math.gcd(q_rows, 128)
    own_first = lax.axis_index("ctx") * q_rows
    ends = []
    end = jnp.int32(0)
    for d in range(lengths_ref.shape[0]):
        end = end + lengths_ref[d]
        ends.append(end - own_first)
    values_t = jnp.transpose(kv_ref[q_rows:])
    for h in range(QH):
        qt_ref[h] = jnp.transpose(q_ref[:, h * HD : (h + 1) * HD])
    for t in range(q_rows // tile):
        keys = (t + 1) * tile
        here = slice(t * tile, (t + 1) * tile)
        row = lax.broadcasted_iota(jnp.int32, (1, tile), 1) + t * tile
        start = jnp.zeros((1, tile), jnp.int32)
        for end in ends:
            start = jnp.where(row >= end, jnp.maximum(start, end), start)
        key = lax.broadcasted_iota(jnp.int32, (keys, tile), 0)
        hidden = (key < start) | (key > row)
        hidden = jnp.concatenate([hidden] * QH, axis=1)
        heads = jnp.concatenate([qt_ref[h, :, here] for h in range(QH)], axis=1)
        scores = jnp.where(hidden, LOW, dot(kv_ref[:keys, :], heads))
        top = jnp.max(scores, axis=0, keepdims=True)
        weights = jnp.exp2((scores - top) * EXP2_SCALE)
        total = jnp.sum(weights, axis=0, keepdims=True)
        mixed = dot(values_t[:, :keys], weights.astype(jnp.bfloat16))
        for h in range(QH):
            part = slice(h * tile, (h + 1) * tile)
            acc_ref[h, :, here] = mixed[:, part]
            stat_ref[h : h + 1, here] = top[:, part]
            stat_ref[QH + h : QH + h + 1, here] = total[:, part]


def past_kernel(distances, is_last, lengths_ref, qt_ref, acc_in, stat_in, *refs):
    kv_refs = refs[: len(distances)]
    acc_ref, stat_ref = refs[len(distances) : len(distances) + 2]
    q_rows = qt_ref.shape[2]
    tile = math.gcd(q_rows, 256)
    half = q_rows // 2
    here = lax.axis_index("ctx")
    odd = here % 2
    own_first = here * q_rows
    first = own_first
    last = own_first
    end = jnp.int32(0)
    for d in range(lengths_ref.shape[0]):
        begin, end = end, end + lengths_ref[d]
        holds = (begin < own_first) & (end > own_first)
        first = jnp.where(holds, begin, first)
        last = jnp.where(holds, end, last)
    live_rows = last - own_first

    def side_by_side(read):
        return jnp.concatenate([read(h) for h in range(QH)], axis=1)

    def absorb(kv_ref, t, skipped=0, cut=None):
        cols = slice(t * tile, (t + 1) * tile)
        live = lax.broadcasted_iota(jnp.int32, (1, tile), 1) + t * tile < live_rows
        live = side_by_side(lambda h: live)
        scores = dot(kv_ref[skipped:q_rows], side_by_side(lambda h: qt_ref[h, :, cols]))
        if cut is not None:
            hidden = lax.broadcasted_iota(jnp.int32, scores.shape, 0) + skipped < cut
            scores = jnp.where(hidden, LOW, scores)
        old_top = side_by_side(lambda h: stat_ref[h : h + 1, cols])
        old_total = side_by_side(lambda h: stat_ref[QH + h : QH + h + 1, cols])
        top = jnp.maximum(old_top, jnp.max(scores, axis=0, keepdims=True))
        top = jnp.where(live, top, old_top)
        weights = jnp.exp2((scores - top) * EXP2_SCALE)
        total = jnp.sum(weights, axis=0, keepdims=True)
        mixed = dot(jnp.transpose(kv_ref[q_rows + skipped :]), weights.astype(jnp.bfloat16))
        decay = jnp.exp2((old_top - top) * EXP2_SCALE)
        total = old_total * decay + jnp.where(live, total, 0.0)
        mixed = jnp.where(live, mixed, 0.0)
        for h in range(QH):
            part = slice(h * tile, (h + 1) * tile)
            acc_ref[h, :, cols] = acc_ref[h, :, cols] * decay[:, part] + mixed[:, part]
            stat_ref[h : h + 1, cols] = top[:, part]
            stat_ref[QH + h : QH + h + 1, cols] = total[:, part]

    for kv_ref, (even_distance, odd_distance) in zip(kv_refs, distances):
        distance = jnp.where(odd == 1, odd_distance, even_distance)
        cut = first - (here - distance) * q_rows
        for t in range(q_rows // tile):
            seen = (distance > 0) & (live_rows > t * tile) & (cut < q_rows)
            pl.when(seen & (cut <= 0))(functools.partial(absorb, kv_ref, t))
            pl.when(seen & (cut > 0) & (cut < half))(
                functools.partial(absorb, kv_ref, t, 0, cut)
            )
            pl.when(seen & (cut >= half))(functools.partial(absorb, kv_ref, t, half, cut))

    if is_last:
        out_ref, mass_ref = refs[len(distances) + 2 :]
        for h in range(QH):
            mixed = acc_ref[h] * (1.0 / stat_ref[QH + h : QH + h + 1, :])
            out_ref[:, h * HD : (h + 1) * HD] = jnp.transpose(mixed.astype(jnp.bfloat16))
        mass_ref[...] = stat_ref[:QH, :] * SCALE + jnp.log(stat_ref[QH:, :])


def state_shapes(q_rows):
    return (
        jax.ShapeDtypeStruct((QH, HD, q_rows), jnp.float32),
        jax.ShapeDtypeStruct((2 * QH, q_rows), jnp.float32),
    )


def own_part(lengths, queries, own):
    q_rows = queries.shape[0]
    in_smem = pl.BlockSpec(memory_space=pltpu.SMEM)
    in_vmem = pl.BlockSpec(memory_space=pltpu.VMEM)
    qt, *state = pl.pallas_call(
        own_kernel,
        out_shape=(jax.ShapeDtypeStruct((QH, HD, q_rows), jnp.bfloat16),) + state_shapes(q_rows),
        in_specs=[in_smem, in_vmem, in_vmem],
        out_specs=(in_vmem, in_vmem, in_vmem),
        compiler_params=pltpu.CompilerParams(vmem_limit_bytes=VMEM_LIMIT),
        cost_estimate=LITTLE,
    )(lengths, queries, own)
    return qt, state


def past_part(lengths, qt, state, shards, is_last=False):
    q_rows = qt.shape[2]
    distances = [s[0] for s in shards]
    arrays = [s[1] for s in shards]
    in_smem = pl.BlockSpec(memory_space=pltpu.SMEM)
    in_vmem = pl.BlockSpec(memory_space=pltpu.VMEM)
    out_shape = state_shapes(q_rows)
    if is_last:
        out_shape += (
            jax.ShapeDtypeStruct((q_rows, QH * HD), jnp.bfloat16),
            jax.ShapeDtypeStruct((QH, q_rows), jnp.float32),
        )
    outs = pl.pallas_call(
        functools.partial(past_kernel, distances, is_last),
        out_shape=out_shape,
        in_specs=[in_smem] + [in_vmem] * (3 + len(arrays)),
        out_specs=(in_vmem,) * len(out_shape),
        input_output_aliases={2: 0, 3: 1},
        compiler_params=pltpu.CompilerParams(vmem_limit_bytes=VMEM_LIMIT),
        cost_estimate=LITTLE,
    )(lengths, qt, *state, *arrays)
    return outs[2:] if is_last else outs


def on_device(lengths, queries, key_rows, values):
    count = lax.axis_size("ctx")
    reach = min(count // 2 + 1, count - 1)
    strides = reach // 2

    def send(value, pairs):
        return lax.ppermute(value, "ctx", pairs)

    own = jnp.concatenate([key_rows, values])
    moving = send(own, [(i, i + 2) for i in range(count - 2)])
    qt, state = own_part(lengths, queries, own)
    own, *state = lax.optimization_barrier((own, *state))
    pairs = [(i, i + 1) for i in range(0, count, 2)]
    if reach % 2 == 1:
        pairs += [(i + 1, i) for i in range(0, count - reach - 1, 2)]
    beside = first_beside = send(own, pairs)
    moving, *state = lax.optimization_barrier((moving, *state))
    side = [((0, 1), beside)]
    for k in range(1, strides + 1):
        arrived = moving
        if k < strides:
            moving = send(arrived, [(i, i + 2) for i in range(2 * k, count - 2)])
        exchange = [(i + 1, i) for i in range(2 * k, count, 2)]
        distances = (2 * k - 1, 0)
        if 2 * k + 1 <= reach:
            exchange += [(i, i + 1) for i in range(2 * k, count, 2)]
            distances = (2 * k - 1, 2 * k + 1)
        shards = [((2 * k, 2 * k), arrived)] + side
        side = [(distances, send(arrived, exchange))]
        state = past_part(lengths, qt, state, shards)
        if k == strides - 1 and reach % 2 == 1:
            first_beside, *state = lax.optimization_barrier((first_beside, *state))
            far = send(first_beside, [(i, i + reach + 1) for i in range(0, count - reach - 1, 2)])
        if k < strides:
            moving, *state = lax.optimization_barrier((moving, *state))
    if reach % 2 == 1:
        side.insert(0, ((reach, 0), far))
    return past_part(lengths, qt, state, side, is_last=True)


def solution(mesh):
    in_specs = (
        P("batch"),
        P(("batch", "ctx"), None),
        P(("batch", "ctx"), None),
        P(("batch", "ctx"), None),
    )
    out_specs = (P(("batch", "ctx"), None), P(None, ("batch", "ctx")))
    return jax.shard_map(
        on_device, mesh=mesh, in_specs=in_specs, out_specs=out_specs, check_vma=False
    )
```

```python
import functools
import math

import jax
import jax.numpy as jnp
from jax import lax
from jax.experimental import pallas as pl
from jax.experimental.pallas import tpu as pltpu
from jax.sharding import PartitionSpec as P

QH = 4
HD = 128
LOW = -1e30
SCALE = 1.0 / math.sqrt(HD)
EXP2_SCALE = SCALE * math.log2(math.e)
VMEM_LIMIT = 32 * 1024 * 1024
LITTLE = pl.CostEstimate(flops=1024, bytes_accessed=1024, transcendentals=0)


def dot(a, b):
    return jnp.dot(a, b, preferred_element_type=jnp.float32)


def own_kernel(lengths_ref, q_ref, kv_ref, qt_ref, acc_ref, stat_ref):
    q_rows = q_ref.shape[0]
    tile = math.gcd(q_rows, 128)
    own_first = lax.axis_index("ctx") * q_rows
    ends = []
    end = jnp.int32(0)
    for d in range(lengths_ref.shape[0]):
        end = end + lengths_ref[d]
        ends.append(end - own_first)
    values_t = jnp.transpose(kv_ref[q_rows:])
    for h in range(QH):
        qt_ref[h] = jnp.transpose(q_ref[:, h * HD : (h + 1) * HD])
    for t in range(q_rows // tile):
        keys = (t + 1) * tile
        here = slice(t * tile, (t + 1) * tile)
        row = lax.broadcasted_iota(jnp.int32, (1, tile), 1) + t * tile
        start = jnp.zeros((1, tile), jnp.int32)
        for end in ends:
            start = jnp.where(row >= end, jnp.maximum(start, end), start)
        key = lax.broadcasted_iota(jnp.int32, (keys, tile), 0)
        hidden = (key < start) | (key > row)
        hidden = jnp.concatenate([hidden] * QH, axis=1)
        heads = jnp.concatenate([qt_ref[h, :, here] for h in range(QH)], axis=1)
        scores = jnp.where(hidden, LOW, dot(kv_ref[:keys, :], heads))
        top = jnp.max(scores, axis=0, keepdims=True)
        weights = jnp.exp2((scores - top) * EXP2_SCALE)
        total = jnp.sum(weights, axis=0, keepdims=True)
        mixed = dot(values_t[:, :keys], weights.astype(jnp.bfloat16))
        for h in range(QH):
            part = slice(h * tile, (h + 1) * tile)
            acc_ref[h, :, here] = mixed[:, part]
            stat_ref[h : h + 1, here] = top[:, part]
            stat_ref[QH + h : QH + h + 1, here] = total[:, part]


def past_kernel(distances, is_last, lengths_ref, qt_ref, acc_in, stat_in, *refs):
    kv_refs = refs[: len(distances)]
    acc_ref, stat_ref = refs[len(distances) : len(distances) + 2]
    q_rows = qt_ref.shape[2]
    half = q_rows // 2
    here = lax.axis_index("ctx")
    odd = here % 2
    own_first = here * q_rows
    first = own_first
    last = own_first
    end = jnp.int32(0)
    for d in range(lengths_ref.shape[0]):
        begin, end = end, end + lengths_ref[d]
        holds = (begin < own_first) & (end > own_first)
        first = jnp.where(holds, begin, first)
        last = jnp.where(holds, end, last)
    live_rows = last - own_first

    def side_by_side(read):
        return jnp.concatenate([read(h) for h in range(QH)], axis=1)

    def absorb(kv_ref, rows, skipped=0, cut=None):
        cols = slice(0, rows)
        live = lax.broadcasted_iota(jnp.int32, (1, rows), 1) < live_rows
        live = side_by_side(lambda h: live)
        scores = dot(kv_ref[skipped:q_rows], side_by_side(lambda h: qt_ref[h, :, cols]))
        if cut is not None:
            hidden = lax.broadcasted_iota(jnp.int32, scores.shape, 0) + skipped < cut
            scores = jnp.where(hidden, LOW, scores)
        old_top = side_by_side(lambda h: stat_ref[h : h + 1, cols])
        old_total = side_by_side(lambda h: stat_ref[QH + h : QH + h + 1, cols])
        top = jnp.maximum(old_top, jnp.max(scores, axis=0, keepdims=True))
        top = jnp.where(live, top, old_top)
        weights = jnp.exp2((scores - top) * EXP2_SCALE)
        total = jnp.sum(weights, axis=0, keepdims=True)
        mixed = dot(jnp.transpose(kv_ref[q_rows + skipped :]), weights.astype(jnp.bfloat16))
        decay = jnp.exp2((old_top - top) * EXP2_SCALE)
        total = old_total * decay + jnp.where(live, total, 0.0)
        mixed = jnp.where(live, mixed, 0.0)
        for h in range(QH):
            part = slice(h * rows, (h + 1) * rows)
            acc_ref[h, :, cols] = acc_ref[h, :, cols] * decay[:, part] + mixed[:, part]
            stat_ref[h : h + 1, cols] = top[:, part]
            stat_ref[QH + h : QH + h + 1, cols] = total[:, part]

    last_pair = here >= lax.axis_size("ctx") - 2
    for kv_ref, (even_distance, odd_distance, only) in zip(kv_refs, distances):
        distance = jnp.where(odd == 1, odd_distance, even_distance)
        cut = first - (here - distance) * q_rows
        seen = (distance > 0) & (live_rows > 0) & (cut < q_rows)
        if only is not None:
            seen = seen & (last_pair == only)
        for rows in (half, q_rows):
            fits = seen & ((live_rows <= half) == (rows == half))
            pl.when(fits & (cut <= 0))(functools.partial(absorb, kv_ref, rows))
            pl.when(fits & (cut > 0) & (cut < half))(
                functools.partial(absorb, kv_ref, rows, 0, cut)
            )
            pl.when(fits & (cut >= half))(functools.partial(absorb, kv_ref, rows, half, cut))

    if is_last:
        out_ref, mass_ref = refs[len(distances) + 2 :]
        for h in range(QH):
            mixed = acc_ref[h] * (1.0 / stat_ref[QH + h : QH + h + 1, :])
            out_ref[:, h * HD : (h + 1) * HD] = jnp.transpose(mixed.astype(jnp.bfloat16))
        mass_ref[...] = stat_ref[:QH, :] * SCALE + jnp.log(stat_ref[QH:, :])


def state_shapes(q_rows):
    return (
        jax.ShapeDtypeStruct((QH, HD, q_rows), jnp.float32),
        jax.ShapeDtypeStruct((2 * QH, q_rows), jnp.float32),
    )


def own_part(lengths, queries, own):
    q_rows = queries.shape[0]
    in_smem = pl.BlockSpec(memory_space=pltpu.SMEM)
    in_vmem = pl.BlockSpec(memory_space=pltpu.VMEM)
    qt, *state = pl.pallas_call(
        own_kernel,
        out_shape=(jax.ShapeDtypeStruct((QH, HD, q_rows), jnp.bfloat16),) + state_shapes(q_rows),
        in_specs=[in_smem, in_vmem, in_vmem],
        out_specs=(in_vmem, in_vmem, in_vmem),
        compiler_params=pltpu.CompilerParams(vmem_limit_bytes=VMEM_LIMIT),
        cost_estimate=LITTLE,
    )(lengths, queries, own)
    return qt, state


def past_part(lengths, qt, state, shards, is_last=False):
    q_rows = qt.shape[2]
    distances = [s[0] for s in shards]
    arrays = [s[1] for s in shards]
    in_smem = pl.BlockSpec(memory_space=pltpu.SMEM)
    in_vmem = pl.BlockSpec(memory_space=pltpu.VMEM)
    out_shape = state_shapes(q_rows)
    if is_last:
        out_shape += (
            jax.ShapeDtypeStruct((q_rows, QH * HD), jnp.bfloat16),
            jax.ShapeDtypeStruct((QH, q_rows), jnp.float32),
        )
    outs = pl.pallas_call(
        functools.partial(past_kernel, distances, is_last),
        out_shape=out_shape,
        in_specs=[in_smem] + [in_vmem] * (3 + len(arrays)),
        out_specs=(in_vmem,) * len(out_shape),
        input_output_aliases={2: 0, 3: 1},
        compiler_params=pltpu.CompilerParams(vmem_limit_bytes=VMEM_LIMIT),
        cost_estimate=LITTLE,
    )(lengths, qt, *state, *arrays)
    return outs[2:] if is_last else outs


def on_device(lengths, queries, key_rows, values):
    count = lax.axis_size("ctx")
    reach = min(count // 2 + 1, count - 1)
    strides = reach // 2

    def send(value, pairs):
        return lax.ppermute(value, "ctx", pairs)

    own = jnp.concatenate([key_rows, values])
    moving = send(own, [(i, i + 2) for i in range(count - 2)])
    qt, state = own_part(lengths, queries, own)
    own, *state = lax.optimization_barrier((own, *state))
    pairs = [(i, i + 1) for i in range(0, count, 2)]
    if reach % 2 == 1:
        pairs += [(i + 1, i) for i in range(0, count - reach - 1, 2)]
    beside = first_beside = send(own, pairs)
    moving, *state = lax.optimization_barrier((moving, *state))
    early, side = [((0, 1, True), beside)], [((0, 1, False), beside)]
    for k in range(1, strides + 1):
        arrived = moving
        if k < strides:
            moving = send(arrived, [(i, i + 2) for i in range(2 * k, count - 2)])
        exchange = [(i + 1, i) for i in range(2 * k, count, 2)]
        distances = (2 * k - 1, 0, None)
        if 2 * k + 1 <= reach:
            exchange += [(i, i + 1) for i in range(2 * k, count, 2)]
            distances = (2 * k - 1, 2 * k + 1, None)
        shards = [((2 * k, 2 * k, None), arrived)] + (early if k == 1 else side)
        side = (side if k == 1 else []) + [(distances, send(arrived, exchange))]
        state = past_part(lengths, qt, state, shards)
        if k == strides - 1 and reach % 2 == 1:
            first_beside, *state = lax.optimization_barrier((first_beside, *state))
            far = send(first_beside, [(i, i + reach + 1) for i in range(0, count - reach - 1, 2)])
        if k < strides:
            moving, *state = lax.optimization_barrier((moving, *state))
    if reach % 2 == 1:
        side.insert(0, ((reach, 0, None), far))
    return past_part(lengths, qt, state, side, is_last=True)


def solution(mesh):
    in_specs = (
        P("batch"),
        P(("batch", "ctx"), None),
        P(("batch", "ctx"), None),
        P(("batch", "ctx"), None),
    )
    out_specs = (P(("batch", "ctx"), None), P(None, ("batch", "ctx")))
    return jax.shard_map(
        on_device, mesh=mesh, in_specs=in_specs, out_specs=out_specs, check_vma=False
    )
```

```python
import functools
import math

import jax
import jax.numpy as jnp
from jax import lax
from jax.experimental import pallas as pl
from jax.experimental.pallas import tpu as pltpu
from jax.sharding import PartitionSpec as P

QH = 4
HD = 128
LOW = -1e30
SCALE = 1.0 / math.sqrt(HD)
EXP2_SCALE = SCALE * math.log2(math.e)
VMEM_LIMIT = 32 * 1024 * 1024
LITTLE = pl.CostEstimate(flops=1024, bytes_accessed=1024, transcendentals=0)


def dot(a, b):
    return jnp.dot(a, b, preferred_element_type=jnp.float32)


def own_kernel(lengths_ref, q_ref, kv_ref, qt_ref, acc_ref, stat_ref):
    q_rows = q_ref.shape[0]
    tile = math.gcd(q_rows, 128)
    own_first = lax.axis_index("ctx") * q_rows
    ends = []
    end = jnp.int32(0)
    for d in range(lengths_ref.shape[0]):
        end = end + lengths_ref[d]
        ends.append(end - own_first)
    values_t = jnp.transpose(kv_ref[q_rows:])
    for h in range(QH):
        qt_ref[h] = jnp.transpose(q_ref[:, h * HD : (h + 1) * HD])
    for t in range(q_rows // tile):
        keys = (t + 1) * tile
        here = slice(t * tile, (t + 1) * tile)
        row = lax.broadcasted_iota(jnp.int32, (1, tile), 1) + t * tile
        start = jnp.zeros((1, tile), jnp.int32)
        for end in ends:
            start = jnp.where(row >= end, jnp.maximum(start, end), start)
        key = lax.broadcasted_iota(jnp.int32, (keys, tile), 0)
        hidden = (key < start) | (key > row)
        hidden = jnp.concatenate([hidden] * QH, axis=1)
        heads = jnp.concatenate([qt_ref[h, :, here] for h in range(QH)], axis=1)
        scores = jnp.where(hidden, LOW, dot(kv_ref[:keys, :], heads))
        top = jnp.max(scores, axis=0, keepdims=True)
        weights = jnp.exp2((scores - top) * EXP2_SCALE)
        total = jnp.sum(weights, axis=0, keepdims=True)
        mixed = dot(values_t[:, :keys], weights.astype(jnp.bfloat16))
        for h in range(QH):
            part = slice(h * tile, (h + 1) * tile)
            acc_ref[h, :, here] = mixed[:, part]
            stat_ref[h : h + 1, here] = top[:, part]
            stat_ref[QH + h : QH + h + 1, here] = total[:, part]


def past_kernel(distances, is_last, lengths_ref, qt_ref, acc_in, stat_in, *refs):
    kv_refs = refs[: len(distances)]
    acc_ref, stat_ref = refs[len(distances) : len(distances) + 2]
    q_rows = qt_ref.shape[2]
    half = q_rows // 2
    here = lax.axis_index("ctx")
    odd = here % 2
    own_first = here * q_rows
    first = own_first
    last = own_first
    end = jnp.int32(0)
    for d in range(lengths_ref.shape[0]):
        begin, end = end, end + lengths_ref[d]
        holds = (begin < own_first) & (end > own_first)
        first = jnp.where(holds, begin, first)
        last = jnp.where(holds, end, last)
    live_rows = last - own_first

    def side_by_side(read):
        return jnp.concatenate([read(h) for h in range(QH)], axis=1)

    def absorb(kv_ref, rows, cols, skipped=0, cut=None):
        live = lax.broadcasted_iota(jnp.int32, (1, rows), 1) + cols.start < live_rows
        live = side_by_side(lambda h: live)
        scores = dot(kv_ref[skipped:q_rows], side_by_side(lambda h: qt_ref[h, :, cols]))
        if cut is not None:
            hidden = lax.broadcasted_iota(jnp.int32, scores.shape, 0) + skipped < cut
            scores = jnp.where(hidden, LOW, scores)
        old_top = side_by_side(lambda h: stat_ref[h : h + 1, cols])
        old_total = side_by_side(lambda h: stat_ref[QH + h : QH + h + 1, cols])
        top = jnp.maximum(old_top, jnp.max(scores, axis=0, keepdims=True))
        top = jnp.where(live, top, old_top)
        weights = jnp.exp2((scores - top) * EXP2_SCALE)
        total = jnp.sum(weights, axis=0, keepdims=True)
        mixed = dot(jnp.transpose(kv_ref[q_rows + skipped :]), weights.astype(jnp.bfloat16))
        decay = jnp.exp2((old_top - top) * EXP2_SCALE)
        total = old_total * decay + jnp.where(live, total, 0.0)
        mixed = jnp.where(live, mixed, 0.0)
        for h in range(QH):
            part = slice(h * rows, (h + 1) * rows)
            acc_ref[h, :, cols] = acc_ref[h, :, cols] * decay[:, part] + mixed[:, part]
            stat_ref[h : h + 1, cols] = top[:, part]
            stat_ref[QH + h : QH + h + 1, cols] = total[:, part]

    def absorb_tiles(kv_ref, skipped, cut):
        def absorb_tile(t, _):
            cols = pl.ds(pl.multiple_of(t * half, half), half)
            absorb(kv_ref, half, cols, skipped, cut)
            return 0

        lax.fori_loop(0, jnp.where(live_rows > half, 2, 1), absorb_tile, 0)

    last_pair = here >= lax.axis_size("ctx") - 2
    for kv_ref, (even_distance, odd_distance, only) in zip(kv_refs, distances):
        distance = jnp.where(odd == 1, odd_distance, even_distance)
        cut = first - (here - distance) * q_rows
        seen = (distance > 0) & (live_rows > 0) & (cut < q_rows)
        if only is not None:
            seen = seen & (last_pair == only)
        wide = (cut <= 0) & (live_rows > half)
        pl.when(seen & wide)(functools.partial(absorb, kv_ref, q_rows, slice(0, q_rows)))
        pl.when(seen & jnp.logical_not(wide) & (cut < half))(
            functools.partial(absorb_tiles, kv_ref, 0, cut)
        )
        pl.when(seen & (cut >= half))(functools.partial(absorb_tiles, kv_ref, half, cut))

    if is_last:
        out_ref, mass_ref = refs[len(distances) + 2 :]
        for h in range(QH):
            mixed = acc_ref[h] * (1.0 / stat_ref[QH + h : QH + h + 1, :])
            out_ref[:, h * HD : (h + 1) * HD] = jnp.transpose(mixed.astype(jnp.bfloat16))
        mass_ref[...] = stat_ref[:QH, :] * SCALE + jnp.log(stat_ref[QH:, :])


def state_shapes(q_rows):
    return (
        jax.ShapeDtypeStruct((QH, HD, q_rows), jnp.float32),
        jax.ShapeDtypeStruct((2 * QH, q_rows), jnp.float32),
    )


def own_part(lengths, queries, own):
    q_rows = queries.shape[0]
    in_smem = pl.BlockSpec(memory_space=pltpu.SMEM)
    in_vmem = pl.BlockSpec(memory_space=pltpu.VMEM)
    qt, *state = pl.pallas_call(
        own_kernel,
        out_shape=(jax.ShapeDtypeStruct((QH, HD, q_rows), jnp.bfloat16),) + state_shapes(q_rows),
        in_specs=[in_smem, in_vmem, in_vmem],
        out_specs=(in_vmem, in_vmem, in_vmem),
        compiler_params=pltpu.CompilerParams(vmem_limit_bytes=VMEM_LIMIT),
        cost_estimate=LITTLE,
    )(lengths, queries, own)
    return qt, state


def past_part(lengths, qt, state, shards, is_last=False):
    q_rows = qt.shape[2]
    distances = [s[0] for s in shards]
    arrays = [s[1] for s in shards]
    in_smem = pl.BlockSpec(memory_space=pltpu.SMEM)
    in_vmem = pl.BlockSpec(memory_space=pltpu.VMEM)
    out_shape = state_shapes(q_rows)
    if is_last:
        out_shape += (
            jax.ShapeDtypeStruct((q_rows, QH * HD), jnp.bfloat16),
            jax.ShapeDtypeStruct((QH, q_rows), jnp.float32),
        )
    outs = pl.pallas_call(
        functools.partial(past_kernel, distances, is_last),
        out_shape=out_shape,
        in_specs=[in_smem] + [in_vmem] * (3 + len(arrays)),
        out_specs=(in_vmem,) * len(out_shape),
        input_output_aliases={2: 0, 3: 1},
        compiler_params=pltpu.CompilerParams(vmem_limit_bytes=VMEM_LIMIT),
        cost_estimate=LITTLE,
    )(lengths, qt, *state, *arrays)
    return outs[2:] if is_last else outs


def on_device(lengths, queries, key_rows, values):
    count = lax.axis_size("ctx")
    reach = min(count // 2 + 1, count - 1)
    strides = reach // 2

    def send(value, pairs):
        return lax.ppermute(value, "ctx", pairs)

    own = jnp.concatenate([key_rows, values])
    moving = send(own, [(i, i + 2) for i in range(count - 2)])
    qt, state = own_part(lengths, queries, own)
    own, *state = lax.optimization_barrier((own, *state))
    pairs = [(i, i + 1) for i in range(0, count, 2)]
    if reach % 2 == 1:
        pairs += [(i + 1, i) for i in range(0, count - reach - 1, 2)]
    beside = first_beside = send(own, pairs)
    moving, *state = lax.optimization_barrier((moving, *state))
    early, side = [((0, 1, True), beside)], [((0, 1, False), beside)]
    for k in range(1, strides + 1):
        arrived = moving
        if k < strides:
            moving = send(arrived, [(i, i + 2) for i in range(2 * k, count - 2)])
        exchange = [(i + 1, i) for i in range(2 * k, count, 2)]
        distances = (2 * k - 1, 0, None)
        if 2 * k + 1 <= reach:
            exchange += [(i, i + 1) for i in range(2 * k, count, 2)]
            distances = (2 * k - 1, 2 * k + 1, None)
        shards = [((2 * k, 2 * k, None), arrived)] + (early if k == 1 else side)
        side = (side if k == 1 else []) + [(distances, send(arrived, exchange))]
        state = past_part(lengths, qt, state, shards)
        if k == strides - 1 and reach % 2 == 1:
            first_beside, *state = lax.optimization_barrier((first_beside, *state))
            far = send(first_beside, [(i, i + reach + 1) for i in range(0, count - reach - 1, 2)])
        if k < strides:
            moving, *state = lax.optimization_barrier((moving, *state))
    if reach % 2 == 1:
        side.insert(0, ((reach, 0, None), far))
    return past_part(lengths, qt, state, side, is_last=True)


def solution(mesh):
    in_specs = (
        P("batch"),
        P(("batch", "ctx"), None),
        P(("batch", "ctx"), None),
        P(("batch", "ctx"), None),
    )
    out_specs = (P(("batch", "ctx"), None), P(None, ("batch", "ctx")))
    return jax.shard_map(
        on_device, mesh=mesh, in_specs=in_specs, out_specs=out_specs, check_vma=False
    )
```

```python
import functools
import math

import jax
import jax.numpy as jnp
from jax import lax
from jax.experimental import pallas as pl
from jax.experimental.pallas import tpu as pltpu
from jax.sharding import PartitionSpec as P

QH = 4
HD = 128
LOW = -1e30
SCALE = 1.0 / math.sqrt(HD)
EXP2_SCALE = SCALE * math.log2(math.e)
MOST_TOTAL = 2.0**64
VMEM_LIMIT = 32 * 1024 * 1024
LITTLE = pl.CostEstimate(flops=1024, bytes_accessed=1024, transcendentals=0)


def dot(a, b):
    return jnp.dot(a, b, preferred_element_type=jnp.float32)


def own_kernel(lengths_ref, q_ref, kv_ref, qt_ref, acc_ref, stat_ref):
    q_rows = q_ref.shape[0]
    tile = math.gcd(q_rows, 128)
    own_first = lax.axis_index("ctx") * q_rows
    ends = []
    end = jnp.int32(0)
    for d in range(lengths_ref.shape[0]):
        end = end + lengths_ref[d]
        ends.append(end - own_first)
    values_t = jnp.transpose(kv_ref[q_rows:])
    for h in range(QH):
        qt_ref[h] = jnp.transpose(q_ref[:, h * HD : (h + 1) * HD])
    for t in range(q_rows // tile):
        keys = (t + 1) * tile
        here = slice(t * tile, (t + 1) * tile)
        row = lax.broadcasted_iota(jnp.int32, (1, tile), 1) + t * tile
        start = jnp.zeros((1, tile), jnp.int32)
        for end in ends:
            start = jnp.where(row >= end, jnp.maximum(start, end), start)
        key = lax.broadcasted_iota(jnp.int32, (keys, tile), 0)
        hidden = (key < start) | (key > row)
        hidden = jnp.concatenate([hidden] * QH, axis=1)
        heads = jnp.concatenate([qt_ref[h, :, here] for h in range(QH)], axis=1)
        scores = jnp.where(hidden, LOW, dot(kv_ref[:keys, :], heads))
        top = jnp.max(scores, axis=0, keepdims=True)
        weights = jnp.exp2((scores - top) * EXP2_SCALE)
        total = jnp.sum(weights, axis=0, keepdims=True)
        mixed = dot(values_t[:, :keys], weights.astype(jnp.bfloat16))
        for h in range(QH):
            part = slice(h * tile, (h + 1) * tile)
            acc_ref[h, :, here] = mixed[:, part]
            stat_ref[h : h + 1, here] = top[:, part]
            stat_ref[QH + h : QH + h + 1, here] = total[:, part]


def past_kernel(distances, is_last, lengths_ref, qt_ref, acc_in, stat_in, *refs):
    kv_refs = refs[: len(distances)]
    acc_ref, stat_ref = refs[len(distances) : len(distances) + 2]
    q_rows = qt_ref.shape[2]
    half = q_rows // 2
    here = lax.axis_index("ctx")
    odd = here % 2
    own_first = here * q_rows
    first = own_first
    last = own_first
    end = jnp.int32(0)
    for d in range(lengths_ref.shape[0]):
        begin, end = end, end + lengths_ref[d]
        holds = (begin < own_first) & (end > own_first)
        first = jnp.where(holds, begin, first)
        last = jnp.where(holds, end, last)
    live_rows = last - own_first

    def side_by_side(read):
        return jnp.concatenate([read(h) for h in range(QH)], axis=1)

    def absorb(kv_ref, rows, cols, skipped=0, cut=None):
        live = lax.broadcasted_iota(jnp.int32, (1, rows), 1) + cols.start < live_rows
        live = side_by_side(lambda h: live)
        scores = dot(kv_ref[skipped:q_rows], side_by_side(lambda h: qt_ref[h, :, cols]))
        if cut is not None:
            hidden = lax.broadcasted_iota(jnp.int32, scores.shape, 0) + skipped < cut
            scores = jnp.where(hidden, LOW, scores)
        old_top = side_by_side(lambda h: stat_ref[h : h + 1, cols])
        old_total = side_by_side(lambda h: stat_ref[QH + h : QH + h + 1, cols])
        top = jnp.maximum(old_top, jnp.max(scores, axis=0, keepdims=True))
        top = jnp.where(live, top, old_top)
        weights = jnp.exp2((scores - top) * EXP2_SCALE)
        total = jnp.sum(weights, axis=0, keepdims=True)
        mixed = dot(jnp.transpose(kv_ref[q_rows + skipped :]), weights.astype(jnp.bfloat16))
        decay = jnp.exp2((old_top - top) * EXP2_SCALE)
        total = old_total * decay + jnp.where(live, total, 0.0)
        mixed = jnp.where(live, mixed, 0.0)
        for h in range(QH):
            part = slice(h * rows, (h + 1) * rows)
            acc_ref[h, :, cols] = acc_ref[h, :, cols] * decay[:, part] + mixed[:, part]
            stat_ref[h : h + 1, cols] = top[:, part]
            stat_ref[QH + h : QH + h + 1, cols] = total[:, part]

    def absorb_tiles(kv_ref, skipped, cut):
        def absorb_tile(t, _):
            cols = pl.ds(pl.multiple_of(t * half, half), half)
            absorb(kv_ref, half, cols, skipped, cut)
            return 0

        lax.fori_loop(0, jnp.where(live_rows > half, 2, 1), absorb_tile, 0)

    def absorb_whole(kv_ref):
        scores = dot(kv_ref[:q_rows], side_by_side(lambda h: qt_ref[h]))
        top = side_by_side(lambda h: stat_ref[h : h + 1, :])
        weights = jnp.exp2((scores - top) * EXP2_SCALE)
        total = jnp.sum(weights, axis=0, keepdims=True)
        mixed = dot(jnp.transpose(kv_ref[q_rows:]), weights.astype(jnp.bfloat16))
        live = lax.broadcasted_iota(jnp.int32, (1, q_rows), 1) < live_rows
        live = side_by_side(lambda h: live)
        total = jnp.where(live, total, 0.0)
        fits = jnp.max(total) < MOST_TOTAL

        @pl.when(fits)
        def _():
            added = jnp.where(live, mixed, 0.0)
            for h in range(QH):
                part = slice(h * q_rows, (h + 1) * q_rows)
                acc_ref[h] += added[:, part]
                stat_ref[QH + h : QH + h + 1, :] += total[:, part]

        return fits

    last_pair = here >= lax.axis_size("ctx") - 2
    for kv_ref, (even_distance, odd_distance, only) in zip(kv_refs, distances):
        distance = jnp.where(odd == 1, odd_distance, even_distance)
        cut = first - (here - distance) * q_rows
        seen = (distance > 0) & (live_rows > 0) & (cut < q_rows)
        if only is not None:
            seen = seen & (last_pair == only)
        wide = seen & (cut <= 0) & (live_rows > half)
        added = lax.cond(
            wide, functools.partial(absorb_whole, kv_ref), lambda: jnp.bool_(False)
        )
        pl.when(seen & jnp.logical_not(added) & (cut < half))(
            functools.partial(absorb_tiles, kv_ref, 0, cut)
        )
        pl.when(seen & (cut >= half))(functools.partial(absorb_tiles, kv_ref, half, cut))

    if is_last:
        out_ref, mass_ref = refs[len(distances) + 2 :]
        for h in range(QH):
            mixed = acc_ref[h] * (1.0 / stat_ref[QH + h : QH + h + 1, :])
            out_ref[:, h * HD : (h + 1) * HD] = jnp.transpose(mixed.astype(jnp.bfloat16))
        mass_ref[...] = stat_ref[:QH, :] * SCALE + jnp.log(stat_ref[QH:, :])


def state_shapes(q_rows):
    return (
        jax.ShapeDtypeStruct((QH, HD, q_rows), jnp.float32),
        jax.ShapeDtypeStruct((2 * QH, q_rows), jnp.float32),
    )


def own_part(lengths, queries, own):
    q_rows = queries.shape[0]
    in_smem = pl.BlockSpec(memory_space=pltpu.SMEM)
    in_vmem = pl.BlockSpec(memory_space=pltpu.VMEM)
    qt, *state = pl.pallas_call(
        own_kernel,
        out_shape=(jax.ShapeDtypeStruct((QH, HD, q_rows), jnp.bfloat16),) + state_shapes(q_rows),
        in_specs=[in_smem, in_vmem, in_vmem],
        out_specs=(in_vmem, in_vmem, in_vmem),
        compiler_params=pltpu.CompilerParams(vmem_limit_bytes=VMEM_LIMIT),
        cost_estimate=LITTLE,
    )(lengths, queries, own)
    return qt, state


def past_part(lengths, qt, state, shards, is_last=False):
    q_rows = qt.shape[2]
    distances = [s[0] for s in shards]
    arrays = [s[1] for s in shards]
    in_smem = pl.BlockSpec(memory_space=pltpu.SMEM)
    in_vmem = pl.BlockSpec(memory_space=pltpu.VMEM)
    out_shape = state_shapes(q_rows)
    if is_last:
        out_shape += (
            jax.ShapeDtypeStruct((q_rows, QH * HD), jnp.bfloat16),
            jax.ShapeDtypeStruct((QH, q_rows), jnp.float32),
        )
    outs = pl.pallas_call(
        functools.partial(past_kernel, distances, is_last),
        out_shape=out_shape,
        in_specs=[in_smem] + [in_vmem] * (3 + len(arrays)),
        out_specs=(in_vmem,) * len(out_shape),
        input_output_aliases={2: 0, 3: 1},
        compiler_params=pltpu.CompilerParams(vmem_limit_bytes=VMEM_LIMIT),
        cost_estimate=LITTLE,
    )(lengths, qt, *state, *arrays)
    return outs[2:] if is_last else outs


def on_device(lengths, queries, key_rows, values):
    count = lax.axis_size("ctx")
    reach = min(count // 2 + 1, count - 1)
    strides = reach // 2

    def send(value, pairs):
        return lax.ppermute(value, "ctx", pairs)

    own = jnp.concatenate([key_rows, values])
    moving = send(own, [(i, i + 2) for i in range(count - 2)])
    qt, state = own_part(lengths, queries, own)
    own, *state = lax.optimization_barrier((own, *state))
    pairs = [(i, i + 1) for i in range(0, count, 2)]
    if reach % 2 == 1:
        pairs += [(i + 1, i) for i in range(0, count - reach - 1, 2)]
    beside = first_beside = send(own, pairs)
    moving, *state = lax.optimization_barrier((moving, *state))
    early, side = [((0, 1, True), beside)], [((0, 1, False), beside)]
    for k in range(1, strides + 1):
        arrived = moving
        if k < strides:
            moving = send(arrived, [(i, i + 2) for i in range(2 * k, count - 2)])
        exchange = [(i + 1, i) for i in range(2 * k, count, 2)]
        distances = (2 * k - 1, 0, None)
        if 2 * k + 1 <= reach:
            exchange += [(i, i + 1) for i in range(2 * k, count, 2)]
            distances = (2 * k - 1, 2 * k + 1, None)
        shards = [((2 * k, 2 * k, None), arrived)] + (early if k == 1 else side)
        side = (side if k == 1 else []) + [(distances, send(arrived, exchange))]
        state = past_part(lengths, qt, state, shards)
        if k == strides - 1 and reach % 2 == 1:
            first_beside, *state = lax.optimization_barrier((first_beside, *state))
            far = send(first_beside, [(i, i + reach + 1) for i in range(0, count - reach - 1, 2)])
        if k < strides:
            moving, *state = lax.optimization_barrier((moving, *state))
    if reach % 2 == 1:
        side.insert(0, ((reach, 0, None), far))
    return past_part(lengths, qt, state, side, is_last=True)


def solution(mesh):
    in_specs = (
        P("batch"),
        P(("batch", "ctx"), None),
        P(("batch", "ctx"), None),
        P(("batch", "ctx"), None),
    )
    out_specs = (P(("batch", "ctx"), None), P(None, ("batch", "ctx")))
    return jax.shard_map(
        on_device, mesh=mesh, in_specs=in_specs, out_specs=out_specs, check_vma=False
    )
```

```python
import functools
import math

import jax
import jax.numpy as jnp
from jax import lax
from jax.experimental import pallas as pl
from jax.experimental.pallas import tpu as pltpu
from jax.sharding import PartitionSpec as P

QH = 4
HD = 128
LOW = -1e30
SCALE = 1.0 / math.sqrt(HD)
EXP2_SCALE = SCALE * math.log2(math.e)
MOST_TOTAL = 2.0**64
FAR = "far"
VMEM_LIMIT = 32 * 1024 * 1024
LITTLE = pl.CostEstimate(flops=1024, bytes_accessed=1024, transcendentals=0)


def dot(a, b):
    return jnp.dot(a, b, preferred_element_type=jnp.float32)


def own_kernel(lengths_ref, q_ref, kv_ref, qt_ref, acc_ref, stat_ref):
    q_rows = q_ref.shape[0]
    tile = math.gcd(q_rows, 128)
    own_first = lax.axis_index("ctx") * q_rows
    ends = []
    end = jnp.int32(0)
    for d in range(lengths_ref.shape[0]):
        end = end + lengths_ref[d]
        ends.append(end - own_first)
    values_t = jnp.transpose(kv_ref[q_rows:])
    for h in range(QH):
        qt_ref[h] = jnp.transpose(q_ref[:, h * HD : (h + 1) * HD])
    for t in range(q_rows // tile):
        keys = (t + 1) * tile
        here = slice(t * tile, (t + 1) * tile)
        row = lax.broadcasted_iota(jnp.int32, (1, tile), 1) + t * tile
        start = jnp.zeros((1, tile), jnp.int32)
        for end in ends:
            start = jnp.where(row >= end, jnp.maximum(start, end), start)
        key = lax.broadcasted_iota(jnp.int32, (keys, tile), 0)
        hidden = (key < start) | (key > row)
        hidden = jnp.concatenate([hidden] * QH, axis=1)
        heads = jnp.concatenate([qt_ref[h, :, here] for h in range(QH)], axis=1)
        scores = jnp.where(hidden, LOW, dot(kv_ref[:keys, :], heads))
        top = jnp.max(scores, axis=0, keepdims=True)
        weights = jnp.exp2((scores - top) * EXP2_SCALE)
        total = jnp.sum(weights, axis=0, keepdims=True)
        mixed = dot(values_t[:, :keys], weights.astype(jnp.bfloat16))
        for h in range(QH):
            part = slice(h * tile, (h + 1) * tile)
            acc_ref[h, :, here] = mixed[:, part]
            stat_ref[h : h + 1, here] = top[:, part]
            stat_ref[QH + h : QH + h + 1, here] = total[:, part]


def past_kernel(distances, is_last, lengths_ref, qt_ref, acc_in, stat_in, *refs):
    kv_refs = refs[: len(distances)]
    acc_ref, stat_ref = refs[len(distances) : len(distances) + 2]
    q_rows = qt_ref.shape[2]
    half = q_rows // 2
    here = lax.axis_index("ctx")
    odd = here % 2
    own_first = here * q_rows
    first = own_first
    last = own_first
    end = jnp.int32(0)
    for d in range(lengths_ref.shape[0]):
        begin, end = end, end + lengths_ref[d]
        holds = (begin < own_first) & (end > own_first)
        first = jnp.where(holds, begin, first)
        last = jnp.where(holds, end, last)
    live_rows = last - own_first

    def side_by_side(read):
        return jnp.concatenate([read(h) for h in range(QH)], axis=1)

    def absorb(kv_ref, rows, cols, skipped=0, cut=None):
        live = lax.broadcasted_iota(jnp.int32, (1, rows), 1) + cols.start < live_rows
        live = side_by_side(lambda h: live)
        scores = dot(kv_ref[skipped:q_rows], side_by_side(lambda h: qt_ref[h, :, cols]))
        if cut is not None:
            hidden = lax.broadcasted_iota(jnp.int32, scores.shape, 0) + skipped < cut
            scores = jnp.where(hidden, LOW, scores)
        old_top = side_by_side(lambda h: stat_ref[h : h + 1, cols])
        old_total = side_by_side(lambda h: stat_ref[QH + h : QH + h + 1, cols])
        top = jnp.maximum(old_top, jnp.max(scores, axis=0, keepdims=True))
        top = jnp.where(live, top, old_top)
        weights = jnp.exp2((scores - top) * EXP2_SCALE)
        total = jnp.sum(weights, axis=0, keepdims=True)
        mixed = dot(jnp.transpose(kv_ref[q_rows + skipped :]), weights.astype(jnp.bfloat16))
        decay = jnp.exp2((old_top - top) * EXP2_SCALE)
        total = old_total * decay + jnp.where(live, total, 0.0)
        mixed = jnp.where(live, mixed, 0.0)
        for h in range(QH):
            part = slice(h * rows, (h + 1) * rows)
            acc_ref[h, :, cols] = acc_ref[h, :, cols] * decay[:, part] + mixed[:, part]
            stat_ref[h : h + 1, cols] = top[:, part]
            stat_ref[QH + h : QH + h + 1, cols] = total[:, part]

    def absorb_tiles(kv_ref, skipped, cut):
        def absorb_tile(t, _):
            cols = pl.ds(pl.multiple_of(t * half, half), half)
            absorb(kv_ref, half, cols, skipped, cut)
            return 0

        lax.fori_loop(0, jnp.where(live_rows > half, 2, 1), absorb_tile, 0)

    def absorb_whole(kv_ref, cut):
        key = lax.broadcasted_iota(jnp.int32, (q_rows, 1), 0)
        scores = dot(kv_ref[:q_rows], side_by_side(lambda h: qt_ref[h]))
        scores = scores + jnp.where(key < cut, LOW, 0.0)
        top = side_by_side(lambda h: stat_ref[h : h + 1, :])
        weights = jnp.exp2((scores - top) * EXP2_SCALE)
        total = jnp.sum(weights, axis=0, keepdims=True)
        mixed = dot(jnp.transpose(kv_ref[q_rows:]), weights.astype(jnp.bfloat16))
        live = lax.broadcasted_iota(jnp.int32, (1, q_rows), 1) < live_rows
        live = side_by_side(lambda h: live)
        total = jnp.where(live, total, 0.0)
        fits = jnp.max(total) < MOST_TOTAL

        @pl.when(fits)
        def _():
            added = jnp.where(live, mixed, 0.0)
            for h in range(QH):
                part = slice(h * q_rows, (h + 1) * q_rows)
                acc_ref[h] += added[:, part]
                stat_ref[QH + h : QH + h + 1, :] += total[:, part]

        return fits

    last_pair = here >= lax.axis_size("ctx") - 2
    for kv_ref, (even_distance, odd_distance, only) in zip(kv_refs, distances):
        distance = jnp.where(odd == 1, odd_distance, even_distance)
        cut = first - (here - distance) * q_rows
        seen = (distance > 0) & (live_rows > 0) & (cut < q_rows)
        if only in (True, False):
            seen = seen & (last_pair == only)
        added = False
        if only != FAR:
            wide = seen & (cut < half) & (live_rows > half)
            whole = functools.partial(absorb_whole, kv_ref, cut)
            added = lax.cond(wide, whole, lambda: jnp.bool_(False))
        pl.when(seen & jnp.logical_not(added) & (cut < half))(
            functools.partial(absorb_tiles, kv_ref, 0, cut)
        )
        pl.when(seen & (cut >= half))(functools.partial(absorb_tiles, kv_ref, half, cut))

    if is_last:
        out_ref, mass_ref = refs[len(distances) + 2 :]
        for h in range(QH):
            mixed = acc_ref[h] * (1.0 / stat_ref[QH + h : QH + h + 1, :])
            out_ref[:, h * HD : (h + 1) * HD] = jnp.transpose(mixed.astype(jnp.bfloat16))
        mass_ref[...] = stat_ref[:QH, :] * SCALE + jnp.log(stat_ref[QH:, :])


def state_shapes(q_rows):
    return (
        jax.ShapeDtypeStruct((QH, HD, q_rows), jnp.float32),
        jax.ShapeDtypeStruct((2 * QH, q_rows), jnp.float32),
    )


def own_part(lengths, queries, own):
    q_rows = queries.shape[0]
    in_smem = pl.BlockSpec(memory_space=pltpu.SMEM)
    in_vmem = pl.BlockSpec(memory_space=pltpu.VMEM)
    qt, *state = pl.pallas_call(
        own_kernel,
        out_shape=(jax.ShapeDtypeStruct((QH, HD, q_rows), jnp.bfloat16),) + state_shapes(q_rows),
        in_specs=[in_smem, in_vmem, in_vmem],
        out_specs=(in_vmem, in_vmem, in_vmem),
        compiler_params=pltpu.CompilerParams(vmem_limit_bytes=VMEM_LIMIT),
        cost_estimate=LITTLE,
    )(lengths, queries, own)
    return qt, state


def past_part(lengths, qt, state, shards, is_last=False):
    q_rows = qt.shape[2]
    distances = [s[0] for s in shards]
    arrays = [s[1] for s in shards]
    in_smem = pl.BlockSpec(memory_space=pltpu.SMEM)
    in_vmem = pl.BlockSpec(memory_space=pltpu.VMEM)
    out_shape = state_shapes(q_rows)
    if is_last:
        out_shape += (
            jax.ShapeDtypeStruct((q_rows, QH * HD), jnp.bfloat16),
            jax.ShapeDtypeStruct((QH, q_rows), jnp.float32),
        )
    outs = pl.pallas_call(
        functools.partial(past_kernel, distances, is_last),
        out_shape=out_shape,
        in_specs=[in_smem] + [in_vmem] * (3 + len(arrays)),
        out_specs=(in_vmem,) * len(out_shape),
        input_output_aliases={2: 0, 3: 1},
        compiler_params=pltpu.CompilerParams(vmem_limit_bytes=VMEM_LIMIT),
        cost_estimate=LITTLE,
    )(lengths, qt, *state, *arrays)
    return outs[2:] if is_last else outs


def on_device(lengths, queries, key_rows, values):
    count = lax.axis_size("ctx")
    reach = min(count // 2 + 1, count - 1)
    strides = reach // 2

    def send(value, pairs):
        return lax.ppermute(value, "ctx", pairs)

    own = jnp.concatenate([key_rows, values])
    moving = send(own, [(i, i + 2) for i in range(count - 2)])
    qt, state = own_part(lengths, queries, own)
    own, *state = lax.optimization_barrier((own, *state))
    pairs = [(i, i + 1) for i in range(0, count, 2)]
    if reach % 2 == 1:
        pairs += [(i + 1, i) for i in range(0, count - reach - 1, 2)]
    beside = first_beside = send(own, pairs)
    moving, *state = lax.optimization_barrier((moving, *state))
    early, side = [((0, 1, True), beside)], [((0, 1, False), beside)]
    for k in range(1, strides + 1):
        arrived = moving
        if k < strides:
            moving = send(arrived, [(i, i + 2) for i in range(2 * k, count - 2)])
        exchange = [(i + 1, i) for i in range(2 * k, count, 2)]
        distances = (2 * k - 1, 0, None)
        if 2 * k + 1 <= reach:
            exchange += [(i, i + 1) for i in range(2 * k, count, 2)]
            distances = (2 * k - 1, 2 * k + 1, None)
        shards = [((2 * k, 2 * k, None), arrived)] + (early if k == 1 else side)
        side = (side if k == 1 else []) + [(distances, send(arrived, exchange))]
        state = past_part(lengths, qt, state, shards)
        if k == strides - 1 and reach % 2 == 1:
            first_beside, *state = lax.optimization_barrier((first_beside, *state))
            far = send(first_beside, [(i, i + reach + 1) for i in range(0, count - reach - 1, 2)])
        if k < strides:
            moving, *state = lax.optimization_barrier((moving, *state))
    if reach % 2 == 1:
        side.insert(0, ((reach, 0, FAR), far))
    return past_part(lengths, qt, state, side, is_last=True)


def solution(mesh):
    in_specs = (
        P("batch"),
        P(("batch", "ctx"), None),
        P(("batch", "ctx"), None),
        P(("batch", "ctx"), None),
    )
    out_specs = (P(("batch", "ctx"), None), P(None, ("batch", "ctx")))
    return jax.shard_map(
        on_device, mesh=mesh, in_specs=in_specs, out_specs=out_specs, check_vma=False
    )
```
